128 devices in a mesh: ctx: 16 (over y_hi, z, core), tp: 8 (over y_lo, x).
Axes of the slice: x: 4, y: 4 (y_hi: 2, y_lo: 2; y = y_hi * 2 + y_lo), z: 4, core: 2. Of those that a mesh axis runs over, the one named last changes fastest.
Arguments:
- queries: bfloat16 [2048, 4096], P('ctx', 'tp'), may hold values from -6 to 6
- keys: bfloat16 [2048, 256], P('ctx'), may hold values from -6 to 6
- values: bfloat16 [2048, 256], P('ctx'), may hold values from -6 to 6
- resid: bfloat16 [2048, 4096], P(('ctx', 'tp')), may hold values from -4 to 4
- out_proj: bfloat16 [4096, 4096], P('tp'), may hold values from -0.375 to 0.375
- norm_gain: float32 [4096], replicated, may hold values from 0.1 to 1.9
- expert_ids: int32 [2048, 8], P(('ctx', 'tp')), may hold values from 0 to 31, all different within a row; in each aligned block of 16 rows (0 to 15, 16 to 31, ...) at most 5 rows name the same one
- gates: float32 [2048, 8], P(('ctx', 'tp')), may hold values from 0.1 to 0.5
- w_gate: bfloat16 [32, 1536, 4096], P('ctx', 'tp'), may hold values from -0.09375 to 0.09375
- w_up: bfloat16 [32, 1536, 4096], P('ctx', 'tp'), may hold values from -0.09375 to 0.09375
- w_down: bfloat16 [32, 1536, 4096], P('ctx', 'tp'), may hold values from -0.15625 to 0.15625
- cotangent: bfloat16 [2048, 4096], P(('ctx', 'tp')), may hold values from -2 to 2
Outputs:
- layer_out: bfloat16 [2048, 4096], P(('ctx', 'tp'))
- grad_gate: bfloat16 [32, 1536, 4096], P('ctx', 'tp')
- grad_up: bfloat16 [32, 1536, 4096], P('ctx', 'tp')
- grad_down: bfloat16 [32, 1536, 4096], P('ctx', 'tp')
The draws below stay inside these ranges and needn't reach their ends.
Inputs may be any that keep to these rules, and one draw needn't show every extreme that they name: `expert_ids`: in the 16 rows of one device (aligned blocks of rows) no expert is named more than 5 times, a bound that some block reaches; each row names 8 different experts.
All inputs are finite; a program needn't handle non-finite values.
Results may differ from the reference program's by a relative error of at most 0.025.
Values may be sent and summed in bfloat16 or wider, within the bound.
No kernel may reach another device: no remote copies, remote signals or barrier semaphores. Data moves between devices by JAX's collectives and lax.ppermute only.
A program may use at most 192 MiB of HBM per device.

```python
import math
import jax
import jax.numpy as jnp
import numpy as np
from jax import lax

D = 4096
FF = 1536
QHEADS = 32
KVHEADS = 2
HEAD = 128
TOPK = 8
ROWS = 16
TOKENS = 2048
EXPERTS = 32
CAP = 5
N_CTX = 16
N_TP = 8


def draw_queries(key, part):
    key = jax.random.fold_in(key, 11)
    drawn = jnp.clip(jax.random.normal(key, (TOKENS, QHEADS, HEAD), jnp.float32), -5.0, 5.0)
    return drawn.reshape(TOKENS, QHEADS * HEAD).astype(jnp.bfloat16)


def draw_keys(key, part):
    key = jax.random.fold_in(key, 12)
    drawn = jnp.clip(jax.random.normal(key, (TOKENS, KVHEADS, HEAD), jnp.float32), -5.0, 5.0)
    return drawn.reshape(TOKENS, KVHEADS * HEAD).astype(jnp.bfloat16)


def steps_of(stream_key, shape, cuts, low, high):
    level, own = 1.0, jax.random.fold_in(stream_key, 6)
    for axis_at, blocks in cuts:
        steps = jnp.exp(jax.random.uniform(jax.random.fold_in(own, axis_at), (blocks,), jnp.float32, low / len(cuts), high / len(cuts)))
        level = level * jnp.repeat(steps, shape[axis_at] // blocks).reshape([-1 if axis == axis_at else 1 for axis in range(len(shape))])
    return level


def assign_block(stream_key, own, number, rows, amount, top, bound, skew):
    ranking = jax.random.permutation(stream_key, amount)
    packed, ordinary = shares(amount, rows * top, bound, skew, True), shares(amount, rows * top, bound, skew, False)
    places = jnp.arange(amount)

    def named(sizes, rotation):
        used = int((sizes > 0).sum())
        fixed = max(1, used // 4)
        passed = fixed + (places - fixed + rotation * (used - fixed)) % max(1, amount - fixed)
        return jnp.zeros((amount,), jnp.int32).at[ranking[jnp.where(places < fixed, places, passed)]].set(jnp.asarray(sizes, jnp.int32))

    sizes = jnp.where(number % 4 == 0, named(packed, number // 4), named(ordinary, number - number // 4 - 1))
    mixed = jax.random.permutation(jax.random.fold_in(own, 3), amount)
    source_of, receiver = mixed[0:amount // 2 * 2:2], mixed[1:amount // 2 * 2:2]
    slack = jnp.minimum(sizes[source_of] - 1, bound - sizes[receiver]) // 2
    slack = jnp.where((source_of == ranking[0]) | (receiver == ranking[0]) | (sizes[receiver] == 0), 0, jnp.maximum(slack, 0))
    passed = jax.random.randint(jax.random.fold_in(own, 4), (amount // 2,), 0, 1 << 20) % (slack + 1)
    sizes = sizes.at[source_of].add(-passed).at[receiver].add(passed)
    items = jnp.searchsorted(jnp.cumsum(sizes), jnp.arange(rows * top), side="right").astype(jnp.int32)
    grid = items.reshape(top, rows).T
    grid = grid[jax.random.permutation(jax.random.fold_in(own, 1), rows)]
    rotation = jax.random.randint(jax.random.fold_in(own, 2), (rows, 1), 0, top)
    return jnp.take_along_axis(grid, (jnp.arange(top)[None, :] + rotation) % top, axis=1)


def shares(count, total, limit, skew, full):
    weights = [(1 << 20) // math.isqrt(grade ** skew) + 1 for grade in range(1, count + 1)]
    largest = limit if full else min(limit, max(-(-total // count), total * weights[0] // sum(weights)))
    least = 1 if total - largest >= count - 1 else 0
    given, rest = [largest] + [least] * (count - 1), total - largest - least * (count - 1)
    while rest > 0:
        free = [i for i in range(1, count) if given[i] < largest] or [i for i in range(1, count) if given[i] < limit]
        pool, remaining = sum([weights[i] for i in free]), rest
        for i in free:
            more = min(limit - given[i], max(1, remaining * weights[i] // pool), rest)
            given[i] = given[i] + more
            rest = rest - more
    return np.array(given)


def gaussian(rng, extent, scale, limit, shards=(), held_as=jnp.bfloat16):
    level = steps_of(rng, extent, shards, -0.22, 0.18) if shards else 1.0
    values = jax.random.normal(rng, extent, jnp.float32) * scale * level
    return jnp.minimum(jnp.maximum(values, -limit), limit).astype(held_as)


def setup_inputs(seed: int = 0) -> dict:
    key_list = jax.random.split(jax.random.key(seed), 13)
    queries = draw_queries(jax.random.fold_in(key_list[12], 71), 0)
    keys = draw_keys(jax.random.fold_in(key_list[12], 71), 0)
    values = gaussian(key_list[2], (TOKENS, KVHEADS * HEAD), 1.0, 6.0, ((0, 16),))
    resid = gaussian(key_list[3], (TOKENS, D), 0.5, 4.0, ((0, 128),))
    out_proj = gaussian(key_list[4], (QHEADS * HEAD, D), (QHEADS * HEAD // 16) ** -0.5, 0.375, ((0, 8),))
    norm_gain = jnp.clip(1.0 + 0.18 * jax.random.normal(key_list[5], (D,), jnp.float32), 0.1, 1.9)
    expert_ids_keys = jax.random.split(jax.random.fold_in(key_list[6], 1), TOKENS // ROWS)
    expert_ids_turns = jax.random.permutation(jax.random.fold_in(key_list[6], 3), TOKENS // ROWS)
    expert_ids = jax.vmap(lambda own, number: assign_block(jax.random.fold_in(key_list[6], 2), own, number, ROWS, EXPERTS, TOPK, CAP, 0))(expert_ids_keys, expert_ids_turns).reshape((TOKENS, TOPK))
    gates = jnp.clip(0.1 + 0.4 * jax.random.uniform(key_list[7], (TOKENS, TOPK), jnp.float32) ** steps_of(key_list[7], (TOKENS, TOPK), ((0, 128),), -0.2, 0.2), 0.1, 0.5)
    w_gate = gaussian(key_list[8], (EXPERTS, FF, D), D ** -0.5, 0.09375, ((0, 16), (1, 8)))
    w_up = gaussian(key_list[9], (EXPERTS, FF, D), D ** -0.5, 0.09375, ((0, 16), (1, 8)))
    w_down = gaussian(key_list[10], (EXPERTS, FF, D), FF ** -0.5, 0.15625, ((0, 16), (1, 8)))
    cotangent = gaussian(key_list[11], (TOKENS, D), 0.3, 2.0, ((0, 128),))
    return {"queries": queries, "keys": keys, "values": values, "resid": resid, "out_proj": out_proj, "norm_gain": norm_gain, "expert_ids": expert_ids, "gates": gates, "w_gate": w_gate, "w_up": w_up, "w_down": w_down, "cotangent": cotangent}


def reference(queries, keys, values, resid, out_proj, norm_gain, expert_ids, gates, w_gate, w_up, w_down, cotangent):
    tokens = queries.shape[0]
    group_size = QHEADS // KVHEADS
    score_scale = 1.0 / math.sqrt(HEAD)
    positions = jnp.arange(tokens, dtype=jnp.int32)
    visible = positions[None, :] <= positions[:, None]

    def one_head(head_index):
        query_head = lax.dynamic_slice_in_dim(queries, head_index * HEAD, HEAD, 1)
        kv_index = head_index // group_size
        key_head = lax.dynamic_slice_in_dim(keys, kv_index * HEAD, HEAD, 1)
        value_head = lax.dynamic_slice_in_dim(values, kv_index * HEAD, HEAD, 1)
        scores = jnp.dot(query_head, key_head.T, preferred_element_type=jnp.float32) * score_scale
        row_max = lax.optimization_barrier(jnp.max(jnp.where(visible, scores, -1e+30), axis=1, keepdims=True))
        probs = jnp.where(visible, jnp.exp(scores - row_max), 0.0)
        output = jnp.dot(probs.astype(jnp.bfloat16), value_head, preferred_element_type=jnp.float32)
        return (output / lax.optimization_barrier(jnp.sum(probs, axis=1, keepdims=True))).astype(jnp.bfloat16)
    heads_out = lax.map(one_head, jnp.arange(QHEADS, dtype=jnp.int32))
    attn = jnp.transpose(heads_out, (1, 0, 2)).reshape(tokens, QHEADS * HEAD)
    stream = resid.astype(jnp.float32) + jnp.dot(attn, out_proj, preferred_element_type=jnp.float32)
    normed = (stream * lax.rsqrt(lax.optimization_barrier(jnp.mean(stream * stream, axis=1, keepdims=True)) + 1e-06) * norm_gain).astype(jnp.bfloat16)
    pad_rows = jnp.concatenate([normed, jnp.zeros((1, D), jnp.bfloat16)], axis=0)
    pad_grads = jnp.concatenate([cotangent.astype(jnp.float32), jnp.zeros((1, D), jnp.float32)], axis=0)
    row_limit = N_CTX * N_TP * CAP
    ff_block = FF // N_TP

    def per_expert(accumulator, expert_index):
        hit_mask = expert_ids == expert_index
        route_weight = lax.optimization_barrier(jnp.sum(jnp.where(hit_mask, gates, 0.0), axis=1))
        chosen = jnp.any(hit_mask, axis=1)
        picked = jnp.nonzero(chosen, size=row_limit, fill_value=tokens)[0].astype(jnp.int32)
        expert_rows = pad_rows[picked]
        row_weight = jnp.concatenate([route_weight, jnp.zeros((1,), jnp.float32)])[picked]
        gate_matrix = lax.dynamic_index_in_dim(w_gate, expert_index, 0, keepdims=False)
        up_matrix = lax.dynamic_index_in_dim(w_up, expert_index, 0, keepdims=False)
        down_matrix = lax.dynamic_index_in_dim(w_down, expert_index, 0, keepdims=False)
        gate_val = jnp.dot(expert_rows, gate_matrix.T, preferred_element_type=jnp.float32)
        up_val = jnp.dot(expert_rows, up_matrix.T, preferred_element_type=jnp.float32)
        sigmoid_val = jax.nn.sigmoid(gate_val)
        silu_val = gate_val * sigmoid_val
        activated = (silu_val * up_val).astype(jnp.bfloat16)
        act_blocks = activated.astype(jnp.float32).reshape(row_limit, N_TP, ff_block)
        down_blocks = down_matrix.astype(jnp.float32).reshape(N_TP, ff_block, D)
        block_out = jnp.einsum('nbf,bfd->nbd', act_blocks, down_blocks, precision=lax.Precision.HIGHEST).astype(jnp.bfloat16)
        block_out = lax.optimization_barrier(block_out)
        expert_out = lax.optimization_barrier(jnp.sum(block_out.astype(jnp.float32), axis=1)).astype(jnp.bfloat16)
        accumulator = accumulator.at[picked].add(row_weight[:, None] * expert_out.astype(jnp.float32))
        grad_rows = (row_weight[:, None] * pad_grads[picked]).astype(jnp.bfloat16)
        back_act = jnp.dot(grad_rows, down_matrix.T, preferred_element_type=jnp.float32)
        d_gate = (back_act * up_val * sigmoid_val * (1.0 + gate_val * (1.0 - sigmoid_val))).astype(jnp.bfloat16)
        d_up = (back_act * silu_val).astype(jnp.bfloat16)
        grad_down = jnp.dot(activated.T, grad_rows, preferred_element_type=jnp.float32).astype(jnp.bfloat16)
        grad_gate = jnp.dot(d_gate.T, expert_rows, preferred_element_type=jnp.float32).astype(jnp.bfloat16)
        grad_up = jnp.dot(d_up.T, expert_rows, preferred_element_type=jnp.float32).astype(jnp.bfloat16)
        return (accumulator, (grad_gate, grad_up, grad_down))
    moe_sum, gradients = lax.scan(per_expert, jnp.zeros((tokens + 1, D), jnp.float32), jnp.arange(EXPERTS, dtype=jnp.int32))
    layer_out = (stream + moe_sum[:tokens]).astype(jnp.bfloat16)
    return (layer_out, gradients[0], gradients[1], gradients[2])
```

```python
import math

import jax
import jax.numpy as jnp
from jax import lax
from jax.experimental import pallas as pl
from jax.experimental.pallas import tpu as pltpu
from jax.sharding import Mesh
from jax.sharding import PartitionSpec as P

QHEADS = 32
KVHEADS = 2
HEAD = 128
TOPK = 8
CAP = 5
ROWS = 16
META = 128
SIZES = (2, 4, 2, 2, 4)
AXES = ("yh", "z", "k", "yl", "x")
VMEM_LIMIT = 56 * 1024 * 1024


def device_index(yh, z, k, yl, x):
    return (((yh * 4 + z) * 2 + k) * 2 + yl) * 4 + x


def shifted(dims, step):
    pairs = []
    for x in range(4):
        for y in range(4):
            for z in range(4):
                for k in range(2):
                    at = {"x": x, "y": y, "z": z}
                    to = dict(at)
                    to[dims[k]] = (to[dims[k]] + step) % 4
                    pairs.append(
                        (
                            device_index(at["y"] // 2, at["z"], k, at["y"] % 2, at["x"]),
                            device_index(to["y"] // 2, to["z"], k, to["y"] % 2, to["x"]),
                        )
                    )
    return pairs


def send(array, dims, step):
    return lax.ppermute(array, AXES, shifted(dims, step))


def swap_cores(array):
    return lax.ppermute(array, "k", [(0, 1), (1, 0)])


def gather_step(block, dims):
    return [block, send(block, dims, 1), send(block, dims, -1), send(block, dims, 2)]


def gather_last(block, dims):
    half = block.shape[0] // 2
    left = send(block, dims, 1)
    right = send(block, dims, -1)
    return block, left, right, send(left[:half], dims, 1), send(right[half:], dims, -1)


ORDERS = ("xyz", "zxy")


def stage_dims(stage):
    return (ORDERS[0][stage], ORDERS[1][stage])


def gather_chips(block):
    for stage in range(2):
        block = jnp.concatenate(gather_step(block, stage_dims(stage)), 0)
    return gather_last(block, stage_dims(2))


def add(*terms):
    total = terms[0].astype(jnp.float32)
    for term in terms[1:]:
        total = total + term.astype(jnp.float32)
    return total


def scatter_chips(mine, left, right, far_a, far_b):
    dims = stage_dims(2)
    half = far_a.shape[0]
    from_right = send(far_a, dims, -1)
    from_left = send(far_b, dims, 1)
    left = jnp.concatenate([add(left[:half], from_right).astype(jnp.bfloat16), left[half:]], 0)
    right = jnp.concatenate([right[:half], add(right[half:], from_left).astype(jnp.bfloat16)], 0)
    total = add(mine, send(left, dims, -1), send(right, dims, 1))
    for stage in (1, 0):
        dims = stage_dims(stage)
        parts = total.astype(jnp.bfloat16).reshape(4, -1, total.shape[1])
        total = add(
            parts[0], send(parts[1], dims, -1), send(parts[2], dims, 1), send(parts[3], dims, -2)
        )
    return total


def placement(meta, experts, me):
    rows = meta.shape[0]
    slots = rows // ROWS * CAP
    turned = meta.astype(jnp.float32).T
    ids = turned[0:TOPK]
    gates = turned[TOPK : 2 * TOPK] + turned[2 * TOPK : 3 * TOPK] + turned[3 * TOPK : 4 * TOPK]
    token = lax.broadcasted_iota(jnp.int32, (rows, rows), 0)
    later = lax.broadcasted_iota(jnp.int32, (rows, rows), 1)
    earlier = ((token // ROWS == later // ROWS) & (token < later)).astype(jnp.float32)
    block = (lax.broadcasted_iota(jnp.int32, (1, rows), 1) // ROWS).astype(jnp.float32)
    slot_at = lax.broadcasted_iota(jnp.int32, (slots, rows), 0).astype(jnp.float32)
    places, weights = [], []
    for side in range(2):
        for local in range(experts):
            expert = ((me ^ side) * experts + local).astype(jnp.float32)
            named = ids == expert
            hit = jnp.max(named.astype(jnp.float32), axis=0, keepdims=True)
            gate = jnp.sum(jnp.where(named, gates, 0.0), axis=0, keepdims=True)
            rank = jnp.dot(
                jnp.broadcast_to(hit, (8, rows)), earlier, preferred_element_type=jnp.float32
            )[0:1]
            slot = jnp.where(hit > 0.0, block * CAP + rank, -1.0)
            place = (slot_at == slot).astype(jnp.float32)
            places.append(place)
            weights.append(jnp.sum(place * gate, axis=1, keepdims=True))
    return jnp.concatenate(places, 0), jnp.concatenate(weights, 0)


def tiles_of(refs):
    mine, left, right, far_a, far_b = refs
    return [mine[...], left[...], right[...], jnp.concatenate([far_a[...], far_b[...]], 0)]


def store_slots(found, tile, own_ref, other_ref):
    slots = found.shape[0] // 4
    span = pl.ds(tile * slots, slots)
    own_ref[0, span, :] = found[0:slots]
    own_ref[1, span, :] = found[slots : 2 * slots]
    other_ref[0, span, :] = found[2 * slots : 3 * slots]
    other_ref[1, span, :] = found[3 * slots :]


def pack_grads_kernel(me_ref, *refs):
    metas, rows = refs[0:5], refs[5:10]
    own_ref, other_ref, place_ref, weight_ref = refs[10:]

    @pl.when(pl.program_id(0) == 0)
    def _():
        for tile, meta in enumerate(tiles_of(metas)):
            place, weight = placement(meta, 2, me_ref[0])
            place_ref[tile] = place.astype(jnp.bfloat16)
            weight_ref[tile] = jnp.broadcast_to(weight, weight_ref.shape[1:])

    for tile, block in enumerate(tiles_of(rows)):
        found = jnp.dot(place_ref[tile], block, preferred_element_type=jnp.float32)
        found = (found * weight_ref[tile][:, 0:1]).astype(jnp.bfloat16)
        store_slots(found, tile, own_ref, other_ref)


def pack_rows_kernel(place_ref, *refs):
    own_ref, other_ref = refs[5:]
    for tile, block in enumerate(tiles_of(refs[0:5])):
        found = jnp.dot(place_ref[tile], block, preferred_element_type=jnp.float32)
        store_slots(found.astype(jnp.bfloat16), tile, own_ref, other_ref)


def merge_kernel(place_ref, weight_ref, own_ref, other_ref, *outs):
    slots = own_ref.shape[1] // 4
    for tile in range(4):
        span = pl.ds(tile * slots, slots)
        block = jnp.concatenate(
            [own_ref[0, span, :], own_ref[1, span, :], other_ref[0, span, :], other_ref[1, span, :]],
            0,
        )
        scaled = (block.astype(jnp.float32) * weight_ref[tile][:, 0:1]).astype(jnp.bfloat16)
        total = lax.dot_general(
            place_ref[tile], scaled, (((0,), (0,)), ((), ())), preferred_element_type=jnp.float32
        ).astype(jnp.bfloat16)
        if tile < 3:
            outs[tile][...] = total
        else:
            half = total.shape[0] // 2
            outs[3][...] = total[:half]
            outs[4][...] = total[half:]


def params():
    return pltpu.CompilerParams(vmem_limit_bytes=VMEM_LIMIT)


def pack_grads(me, parts, width, chunk):
    part_rows = [part.shape[0] for part in parts]
    tile_rows = part_rows[0]
    slots = tile_rows // ROWS * CAP
    meta_at = width // META
    metas = [pl.BlockSpec((n, META), lambda j: (0, meta_at)) for n in part_rows]
    blocks = [pl.BlockSpec((n, chunk), lambda j: (0, j)) for n in part_rows]
    out_block = pl.BlockSpec((2, 4 * slots, chunk), lambda j: (0, 0, j))
    return pl.pallas_call(
        pack_grads_kernel,
        grid=(width // chunk,),
        in_specs=[pl.BlockSpec(memory_space=pltpu.SMEM)] + metas + blocks,
        out_specs=[
            out_block,
            out_block,
            pl.BlockSpec((4, 4 * slots, tile_rows), lambda j: (0, 0, 0)),
            pl.BlockSpec((4, 4 * slots, META), lambda j: (0, 0, 0)),
        ],
        out_shape=[
            jax.ShapeDtypeStruct((2, 4 * slots, width), jnp.bfloat16),
            jax.ShapeDtypeStruct((2, 4 * slots, width), jnp.bfloat16),
            jax.ShapeDtypeStruct((4, 4 * slots, tile_rows), jnp.bfloat16),
            jax.ShapeDtypeStruct((4, 4 * slots, META), jnp.float32),
        ],
        compiler_params=params(),
    )(me, *parts, *parts)


def pack_rows(place, parts, chunk):
    width = parts[0].shape[1]
    slots = place.shape[1] // 4
    blocks = [pl.BlockSpec((part.shape[0], chunk), lambda j: (0, j)) for part in parts]
    out_block = pl.BlockSpec((2, 4 * slots, chunk), lambda j: (0, 0, j))
    return pl.pallas_call(
        pack_rows_kernel,
        grid=(width // chunk,),
        in_specs=[pl.BlockSpec(place.shape, lambda j: (0, 0, 0))] + blocks,
        out_specs=[out_block, out_block],
        out_shape=[jax.ShapeDtypeStruct((2, 4 * slots, width), jnp.bfloat16)] * 2,
        compiler_params=params(),
    )(place, *parts)


def merge(place, weight, own, other, chunk):
    width = own.shape[2]
    rows = place.shape[2]
    slot_block = pl.BlockSpec((2, own.shape[1], chunk), lambda j: (0, 0, j))
    sizes = [rows, rows, rows, rows // 2, rows // 2]
    return pl.pallas_call(
        merge_kernel,
        grid=(width // chunk,),
        in_specs=[
            pl.BlockSpec(place.shape, lambda j: (0, 0, 0)),
            pl.BlockSpec(weight.shape, lambda j: (0, 0, 0)),
            slot_block,
            slot_block,
        ],
        out_specs=[pl.BlockSpec((n, chunk), lambda j: (0, j)) for n in sizes],
        out_shape=[jax.ShapeDtypeStruct((n, width), jnp.bfloat16) for n in sizes],
        compiler_params=params(),
    )(place, weight, own, other)


def dot_t(a, b):
    return lax.dot_general(a, b, (((1,), (1,)), ((), ())), preferred_element_type=jnp.float32)


def t_dot(a, b):
    return lax.dot_general(a, b, (((0,), (0,)), ((), ())), preferred_element_type=jnp.float32)


def forward_kernel(own_ref, other_ref, wg_ref, wu_ref, wd_ref, *outs):
    for side, rows_ref in enumerate((own_ref, other_ref)):
        out_ref, hidden_ref = outs[side], outs[2]
        gate = dot_t(rows_ref[0], wg_ref[0])
        up = dot_t(rows_ref[0], wu_ref[0])
        hidden_ref[0, side, 0] = gate
        hidden_ref[0, side, 1] = up
        active = (gate * jax.nn.sigmoid(gate) * up).astype(jnp.bfloat16)
        out_ref[0] = jnp.dot(active, wd_ref[0], preferred_element_type=jnp.float32).astype(
            jnp.bfloat16
        )


def forward(own, other, w_gate, w_up, w_down):
    experts, rows, width = own.shape
    hidden = w_gate.shape[1]
    row_block = pl.BlockSpec((1, rows, width), lambda e: (e, 0, 0))
    weight_block = pl.BlockSpec((1, hidden, width), lambda e: (e, 0, 0))
    return pl.pallas_call(
        forward_kernel,
        grid=(experts,),
        in_specs=[row_block, row_block, weight_block, weight_block, weight_block],
        out_specs=[
            row_block,
            row_block,
            pl.BlockSpec((1, 2, 2, rows, hidden), lambda e: (e, 0, 0, 0, 0)),
        ],
        out_shape=[
            jax.ShapeDtypeStruct(own.shape, jnp.bfloat16),
            jax.ShapeDtypeStruct(own.shape, jnp.bfloat16),
            jax.ShapeDtypeStruct((experts, 2, 2, rows, hidden), jnp.float32),
        ],
        compiler_params=params(),
    )(own, other, w_gate, w_up, w_down)


def backward_kernel(
    own_ref, other_ref, gown_ref, gother_ref, wd_ref, hidden_ref, dg_ref, du_ref, dd_ref
):
    d_gates, d_ups, actives = [], [], []
    for side, grads_ref in enumerate((gown_ref, gother_ref)):
        gate, up = hidden_ref[0, side, 0], hidden_ref[0, side, 1]
        sig = jax.nn.sigmoid(gate)
        silu = gate * sig
        back = dot_t(grads_ref[0], wd_ref[0])
        actives.append((silu * up).astype(jnp.bfloat16))
        d_gates.append((back * up * sig * (1.0 + gate * (1.0 - sig))).astype(jnp.bfloat16))
        d_ups.append((back * silu).astype(jnp.bfloat16))
    dd = t_dot(actives[0], gown_ref[0]) + t_dot(actives[1], gother_ref[0])
    dd_ref[0] = dd.astype(jnp.bfloat16)
    dg = t_dot(d_gates[0], own_ref[0]) + t_dot(d_gates[1], other_ref[0])
    dg_ref[0] = dg.astype(jnp.bfloat16)
    du = t_dot(d_ups[0], own_ref[0]) + t_dot(d_ups[1], other_ref[0])
    du_ref[0] = du.astype(jnp.bfloat16)


def backward(own, other, gown, gother, w_down, hidden):
    experts, rows, width = own.shape
    units = w_down.shape[1]
    row_block = pl.BlockSpec((1, rows, width), lambda e: (e, 0, 0))
    weight_block = pl.BlockSpec((1, units, width), lambda e: (e, 0, 0))
    return pl.pallas_call(
        backward_kernel,
        grid=(experts,),
        in_specs=[row_block] * 4
        + [weight_block, pl.BlockSpec((1, 2, 2, rows, units), lambda e: (e, 0, 0, 0, 0))],
        out_specs=[weight_block] * 3,
        out_shape=[jax.ShapeDtypeStruct(w_down.shape, jnp.bfloat16)] * 3,
        compiler_params=params(),
    )(own, other, gown, gother, w_down, hidden)


def gather_keys(pair):
    block = jnp.concatenate([pair, lax.ppermute(pair, "yh", [(0, 1), (1, 0)])], 0)
    block = jnp.concatenate(gather_step(block, "zz"), 0)
    return jnp.concatenate([block, swap_cores(block)], 0)


def key_positions(tok_ctx):
    yh, z, k = (lax.axis_index(name) for name in ("yh", "z", "k"))
    starts = []
    for flip_k in range(2):
        for dz in (0, 3, 1, 2):
            for flip_y in range(2):
                starts.append((((yh ^ flip_y) * 4 + (z + dz) % 4) * 2 + (k ^ flip_k)) * tok_ctx)
    starts = jnp.stack(starts).astype(jnp.int32)
    return (starts[:, None] + jnp.arange(tok_ctx, dtype=jnp.int32)[None, :]).reshape(-1)


def shards(
    queries,
    keys,
    values,
    resid,
    out_proj,
    norm_gain,
    expert_ids,
    gates,
    w_gate,
    w_up,
    w_down,
    cotangent,
):
    width = resid.shape[1]
    chunk = min(512, width)
    yh, z, k, yl = (lax.axis_index(name) for name in ("yh", "z", "k", "yl"))
    ctx = ((yh * 4 + z) * 2 + k).astype(jnp.int32)

    tok_ctx = queries.shape[0]
    heads_dev = queries.shape[1] // HEAD
    key_mine = lax.dynamic_slice_in_dim(keys, yl * HEAD, HEAD, 1)
    value_mine = lax.dynamic_slice_in_dim(values, yl * HEAD, HEAD, 1)
    pairs = gather_keys(jnp.concatenate([key_mine, value_mine], 1))

    rest = gates
    pieces = [expert_ids.astype(jnp.bfloat16)]
    for _ in range(3):
        piece = lax.reduce_precision(rest, 8, 7)
        pieces.append(piece.astype(jnp.bfloat16))
        rest = rest - piece
    pieces.append(jnp.zeros((ROWS, META - 4 * TOPK), jnp.bfloat16))
    cot_parts = gather_chips(jnp.concatenate([cotangent] + pieces, 1))
    me = ctx.reshape(1)
    grads_own, grads_other, place, weight = pack_grads(me, cot_parts, width, chunk)
    grads_got = swap_cores(grads_other)

    key_all, value_all = pairs[:, :HEAD], pairs[:, HEAD:]
    query_pos = ctx * tok_ctx + jnp.arange(tok_ctx, dtype=jnp.int32)
    query_heads = queries.reshape(tok_ctx, heads_dev, HEAD)
    scores = jnp.einsum(
        "qhd,kd->hqk", query_heads, key_all, preferred_element_type=jnp.float32
    ) * (1.0 / math.sqrt(HEAD))
    visible = key_positions(tok_ctx)[None, None, :] <= query_pos[None, :, None]
    top = jnp.max(jnp.where(visible, scores, -1e30), axis=2)
    probs = jnp.where(visible, jnp.exp(scores - top[:, :, None]), 0.0)
    denom = jnp.sum(probs, axis=2)
    heads_out = jnp.einsum(
        "hqk,kd->hqd", probs.astype(jnp.bfloat16), value_all, preferred_element_type=jnp.float32
    )
    heads_out = (heads_out / denom[:, :, None]).astype(jnp.bfloat16)
    attn = jnp.transpose(heads_out, (1, 0, 2)).reshape(tok_ctx, heads_dev * HEAD)
    mixed = jnp.dot(attn, out_proj, preferred_element_type=jnp.float32).astype(jnp.bfloat16)
    mixed = lax.all_to_all(mixed, ("yl", "x"), 0, 0, tiled=True).reshape(8, ROWS, width)
    stream = resid.astype(jnp.float32) + jnp.sum(mixed.astype(jnp.float32), axis=0)
    normed = (
        stream * lax.rsqrt(jnp.mean(stream * stream, axis=1, keepdims=True) + 1e-06) * norm_gain
    ).astype(jnp.bfloat16)

    row_parts = gather_chips(normed)
    rows_own, rows_other = pack_rows(place, row_parts, chunk)
    rows_got = swap_cores(rows_other)
    out_own, out_other, hidden = forward(rows_own, rows_got, w_gate, w_up, w_down)
    out_got = swap_cores(out_other)
    sums = merge(place, weight, out_own, out_got, chunk)
    grad_gate, grad_up, grad_down = backward(
        rows_own, rows_got, grads_own, grads_got, w_down, hidden
    )
    combined = scatter_chips(*sums)
    layer_out = (stream + combined).astype(jnp.bfloat16)
    return layer_out, grad_gate, grad_up, grad_down


def solution(mesh):
    split = Mesh(mesh.devices.reshape(SIZES), AXES)
    ctx, tp = ("yh", "z", "k"), ("yl", "x")
    rows, weights = P(ctx + tp, None), P(ctx, tp, None)
    in_specs = (
        P(ctx, tp),
        P(ctx, None),
        P(ctx, None),
        rows,
        P(tp, None),
        P(),
        rows,
        rows,
        weights,
        weights,
        weights,
        rows,
    )
    return jax.shard_map(
        shards,
        mesh=split,
        in_specs=in_specs,
        out_specs=(rows, weights, weights, weights),
        check_vma=False,
    )
```

```python
import math

import jax
import jax.numpy as jnp
from jax import lax
from jax.experimental import pallas as pl
from jax.experimental.pallas import tpu as pltpu
from jax.sharding import Mesh
from jax.sharding import PartitionSpec as P

QHEADS = 32
KVHEADS = 2
HEAD = 128
TOPK = 8
CAP = 5
ROWS = 16
META = 128
SIZES = (2, 4, 2, 2, 4)
AXES = ("yh", "z", "k", "yl", "x")


def device_index(yh, z, k, yl, x):
    return (((yh * 4 + z) * 2 + k) * 2 + yl) * 4 + x


def shifted(dims, step):
    pairs = []
    for x in range(4):
        for y in range(4):
            for z in range(4):
                for k in range(2):
                    at = {"x": x, "y": y, "z": z}
                    to = dict(at)
                    to[dims[k]] = (to[dims[k]] + step) % 4
                    pairs.append(
                        (
                            device_index(at["y"] // 2, at["z"], k, at["y"] % 2, at["x"]),
                            device_index(to["y"] // 2, to["z"], k, to["y"] % 2, to["x"]),
                        )
                    )
    return pairs


def send(array, dims, step):
    return lax.ppermute(array, AXES, shifted(dims, step))


def swap_cores(array):
    return lax.ppermute(array, "k", [(0, 1), (1, 0)])


def gather_step(block, dims):
    return [block, send(block, dims, 1), send(block, dims, -1), send(block, dims, 2)]


ORDERS = ("xyz", "zxy")


def stage_dims(stage):
    return (ORDERS[0][stage], ORDERS[1][stage])


def after(array, *others):
    return lax.optimization_barrier((array,) + others)[0]


def after_all(arrays, *others):
    return tuple(after(array, *others) for array in arrays)


def gather_near(block):
    for stage in range(2):
        block = jnp.concatenate(gather_step(block, stage_dims(stage)), 0)
    return block


def gather_sides(block):
    dims = stage_dims(2)
    return send(block, dims, 1), send(block, dims, -1)


def gather_far(left, right):
    dims = stage_dims(2)
    half = left.shape[0] // 2
    return send(left[:half], dims, 1), send(right[half:], dims, -1)


def add(*terms):
    total = terms[0].astype(jnp.float32)
    for term in terms[1:]:
        total = total + term.astype(jnp.float32)
    return total


def scatter_near(total):
    for stage in (1, 0):
        dims = stage_dims(stage)
        parts = total.astype(jnp.bfloat16).reshape(4, -1, total.shape[1])
        total = add(
            parts[0], send(parts[1], dims, -1), send(parts[2], dims, 1), send(parts[3], dims, -2)
        )
    return total


def placement(meta, experts, me):
    rows = meta.shape[0]
    slots = rows // ROWS * CAP
    turned = meta.astype(jnp.float32).T
    ids = turned[0:TOPK]
    gates = turned[TOPK : 2 * TOPK] + turned[2 * TOPK : 3 * TOPK] + turned[3 * TOPK : 4 * TOPK]
    token = lax.broadcasted_iota(jnp.int32, (rows, rows), 0)
    later = lax.broadcasted_iota(jnp.int32, (rows, rows), 1)
    earlier = ((token // ROWS == later // ROWS) & (token < later)).astype(jnp.float32)
    block = (lax.broadcasted_iota(jnp.int32, (1, rows), 1) // ROWS).astype(jnp.float32)
    slot_at = lax.broadcasted_iota(jnp.int32, (slots, rows), 0).astype(jnp.float32)
    places, weights = [], []
    for side in range(2):
        for local in range(experts):
            expert = ((me ^ side) * experts + local).astype(jnp.float32)
            named = ids == expert
            hit = jnp.max(named.astype(jnp.float32), axis=0, keepdims=True)
            gate = jnp.sum(jnp.where(named, gates, 0.0), axis=0, keepdims=True)
            rank = jnp.dot(
                jnp.broadcast_to(hit, (8, rows)), earlier, preferred_element_type=jnp.float32
            )[0:1]
            slot = jnp.where(hit > 0.0, block * CAP + rank, -1.0)
            place = (slot_at == slot).astype(jnp.float32)
            places.append(place)
            weights.append(jnp.sum(place * gate, axis=1, keepdims=True))
    return jnp.concatenate(places, 0), jnp.concatenate(weights, 0)


def cost(flops, *arrays):
    moved = sum(array.size * array.dtype.itemsize for array in arrays)
    return pl.CostEstimate(flops=int(flops), bytes_accessed=int(moved), transcendentals=0)


def call(kernel, grid, ins, in_specs, outs, out_specs, flops, scratch=(), limit=24, told=False):
    return pl.pallas_call(
        kernel,
        grid=grid,
        in_specs=in_specs,
        out_specs=out_specs,
        out_shape=outs,
        scratch_shapes=list(scratch),
        compiler_params=pltpu.CompilerParams(vmem_limit_bytes=limit * 1024 * 1024),
        cost_estimate=cost(flops, *ins, *outs) if told else None,
    )(*ins)


def shape(dims, dtype=jnp.bfloat16):
    return jax.ShapeDtypeStruct(dims, dtype)


def joined(refs):
    return refs[0][...] if len(refs) == 1 else jnp.concatenate([ref[...] for ref in refs], 0)


def store_slots(found, tile, own_ref, other_ref):
    slots = found.shape[0] // 4
    span = pl.ds(tile * slots, slots)
    own_ref[0, span, :] = found[0:slots]
    own_ref[1, span, :] = found[slots : 2 * slots]
    other_ref[0, span, :] = found[2 * slots : 3 * slots]
    other_ref[1, span, :] = found[3 * slots :]


def pack_rows(me, groups, width, chunk):
    parts = [part for group in groups for part in group]
    tile_rows = sum(part.shape[0] for part in groups[0])
    slots = tile_rows // ROWS * CAP
    count, total = len(groups), len(parts)
    meta_at = width // META

    def kernel(me_ref, *refs):
        metas, rows = refs[:total], refs[total : 2 * total]
        own_ref, other_ref, place_ref, weight_ref = refs[2 * total :]

        @pl.when(pl.program_id(0) == 0)
        def _():
            at = 0
            for tile, group in enumerate(groups):
                meta = joined(metas[at : at + len(group)])
                at += len(group)
                place, weight = placement(meta, 2, me_ref[0])
                place_ref[tile] = place.astype(jnp.bfloat16)
                weight_ref[tile] = jnp.broadcast_to(weight, weight_ref.shape[1:])

        at = 0
        for tile, group in enumerate(groups):
            block = joined(rows[at : at + len(group)])
            at += len(group)
            found = jnp.dot(place_ref[tile], block, preferred_element_type=jnp.float32)
            store_slots(found.astype(jnp.bfloat16), tile, own_ref, other_ref)

    out_block = pl.BlockSpec((2, count * slots, chunk), lambda j: (0, 0, j))
    return call(
        kernel,
        (width // chunk,),
        (me, *parts, *parts),
        [pl.BlockSpec(memory_space=pltpu.SMEM)]
        + [pl.BlockSpec((part.shape[0], META), lambda j: (0, meta_at)) for part in parts]
        + [pl.BlockSpec((part.shape[0], chunk), lambda j: (0, j)) for part in parts],
        [shape((2, count * slots, width))] * 2
        + [
            shape((count, 4 * slots, tile_rows)),
            shape((count, 4 * slots, META), jnp.float32),
        ],
        [out_block, out_block]
        + [
            pl.BlockSpec((count, 4 * slots, tile_rows), lambda j: (0, 0, 0)),
            pl.BlockSpec((count, 4 * slots, META), lambda j: (0, 0, 0)),
        ],
        2 * count * 4 * slots * tile_rows * width,
    )


def pack_grads(places, weights, tiles, chunk):
    parts = [part for group in tiles for part in group]
    width = parts[0].shape[1]
    tile_rows = places[0].shape[2]
    slots = places[0].shape[1] // 4
    count = len(places)

    def kernel(*refs):
        place_refs, weight_refs = refs[:count], refs[count : 2 * count]
        rows, (own_ref, other_ref) = refs[2 * count : -2], refs[-2:]
        placed = [ref[t] for ref in place_refs for t in range(ref.shape[0])]
        scales = [ref[t] for ref in weight_refs for t in range(ref.shape[0])]
        at = 0
        for tile, group in enumerate(tiles):
            block = joined(rows[at : at + len(group)])
            at += len(group)
            found = jnp.dot(placed[tile], block, preferred_element_type=jnp.float32)
            found = (found * scales[tile][:, 0:1]).astype(jnp.bfloat16)
            store_slots(found, tile, own_ref, other_ref)

    out_block = pl.BlockSpec((2, len(tiles) * slots, chunk), lambda j: (0, 0, j))
    return call(
        kernel,
        (width // chunk,),
        (*places, *weights, *parts),
        [pl.BlockSpec(a.shape, lambda j: (0, 0, 0)) for a in (*places, *weights)]
        + [pl.BlockSpec((part.shape[0], chunk), lambda j: (0, j)) for part in parts],
        [shape((2, len(tiles) * slots, width))] * 2,
        [out_block, out_block],
        2 * len(tiles) * 4 * slots * tile_rows * width,
        told=True,
    )


def merge(place, weight, own, other, pieces, chunk, into=()):
    width = own.shape[2]
    rows = place.shape[2]
    slots = place.shape[1] // 4
    count = own.shape[1] // slots

    def kernel(place_ref, weight_ref, own_ref, other_ref, *refs):
        outs = refs[len(into) :]
        totals = []
        for tile in range(count):
            span = pl.ds(tile * slots, slots)
            block = jnp.concatenate(
                [ref[e, span, :] for ref in (own_ref, other_ref) for e in range(2)], 0
            )
            scale = weight_ref[tile][:, 0:1]
            scaled = (block.astype(jnp.float32) * scale).astype(jnp.bfloat16)
            totals.append(t_dot(place_ref[tile], scaled).astype(jnp.bfloat16))
        at = 0
        for out, (size, _, _) in zip(outs, pieces):
            out[...] = totals[at // rows][at % rows : at % rows + size]
            at += size

    slot_block = pl.BlockSpec((2, own.shape[1], chunk), lambda j: (0, 0, j))
    return pl.pallas_call(
        kernel,
        grid=(width // chunk,),
        in_specs=[
            pl.BlockSpec(place.shape, lambda j: (0, 0, 0)),
            pl.BlockSpec(weight.shape, lambda j: (0, 0, 0)),
            slot_block,
            slot_block,
        ]
        + [pl.BlockSpec(memory_space=pl.ANY)] * len(into),
        out_specs=[
            pl.BlockSpec((size, chunk), lambda j, at=at: (at, j)) for size, _, at in pieces
        ],
        out_shape=[shape((total, width)) for _, total, _ in pieces],
        input_output_aliases={4 + i: i for i in range(len(into))},
        compiler_params=pltpu.CompilerParams(vmem_limit_bytes=24 * 1024 * 1024),
    )(place, weight, own, other, *into)


def dot_t(a, b):
    return lax.dot_general(a, b, (((1,), (1,)), ((), ())), preferred_element_type=jnp.float32)


def t_dot(a, b):
    return lax.dot_general(a, b, (((0,), (0,)), ((), ())), preferred_element_type=jnp.float32)


def forward(own, other, w_gate, w_up, w_down, chunk):
    experts, rows, width = own.shape
    hidden = w_gate.shape[1]
    steps = width // chunk

    def kernel(own_ref, other_ref, wg_ref, wu_ref, wd_ref, *rest):
        own_out, other_out, hidden_ref, gate_sum, up_sum, active_ref = rest
        step = pl.program_id(1)

        @pl.when(step < steps)
        def _():
            block = jnp.concatenate([own_ref[0], other_ref[0]], 0)
            gate = dot_t(block, wg_ref[0])
            up = dot_t(block, wu_ref[0])

            @pl.when(step == 0)
            def _():
                gate_sum[...] = gate
                up_sum[...] = up

            @pl.when(step > 0)
            def _():
                gate_sum[...] += gate
                up_sum[...] += up

        @pl.when(step == steps)
        def _():
            gate, up = gate_sum[...], up_sum[...]
            hidden_ref[0, 0] = gate
            hidden_ref[0, 1] = up
            active_ref[...] = (gate * jax.nn.sigmoid(gate) * up).astype(jnp.bfloat16)

        @pl.when(step >= steps)
        def _():
            out = jnp.dot(active_ref[...], wd_ref[0], preferred_element_type=jnp.float32)
            out = out.astype(jnp.bfloat16)
            own_out[0] = out[:rows]
            other_out[0] = out[rows:]

    def early(e, s):
        return (e, 0, jnp.minimum(s, steps - 1))

    def late(e, s):
        return (e, 0, jnp.maximum(s - steps, 0))

    row_block = pl.BlockSpec((1, rows, chunk), early)
    weight_block = pl.BlockSpec((1, hidden, chunk), early)
    return call(
        kernel,
        (experts, 2 * steps),
        (own, other, w_gate, w_up, w_down),
        [row_block, row_block, weight_block, weight_block, pl.BlockSpec((1, hidden, chunk), late)],
        [shape(own.shape), shape(own.shape), shape((experts, 2, 2 * rows, hidden), jnp.float32)],
        [
            pl.BlockSpec((1, rows, chunk), late),
            pl.BlockSpec((1, rows, chunk), late),
            pl.BlockSpec((1, 2, 2 * rows, hidden), lambda e, s: (e, 0, 0, 0)),
        ],
        12 * experts * rows * hidden * width,
        [
            pltpu.VMEM((2 * rows, hidden), jnp.float32),
            pltpu.VMEM((2 * rows, hidden), jnp.float32),
            pltpu.VMEM((2 * rows, hidden), jnp.bfloat16),
        ],
    )


def back_act(grads, w_down, chunk):
    experts, rows, width = grads[0].shape
    hidden = w_down.shape[1]

    def kernel(own_ref, other_ref, wd_ref, out_ref):
        block = jnp.concatenate([own_ref[0], other_ref[0]], 0)
        found = dot_t(block, wd_ref[0])

        @pl.when(pl.program_id(1) == 0)
        def _():
            out_ref[0] = found

        @pl.when(pl.program_id(1) > 0)
        def _():
            out_ref[0] += found

    row_block = pl.BlockSpec((1, rows, chunk), lambda e, s: (e, 0, s))
    return call(
        kernel,
        (experts, width // chunk),
        (*grads, w_down),
        [row_block, row_block, pl.BlockSpec((1, hidden, chunk), lambda e, s: (e, 0, s))],
        [shape((experts, 2 * rows, hidden), jnp.float32)],
        [pl.BlockSpec((1, 2 * rows, hidden), lambda e, s: (e, 0, 0))],
        4 * experts * rows * hidden * width,
        told=True,
    )[0]


def hidden_of(refs, which):
    halves = [[], []]
    for ref in refs:
        rows = ref.shape[2] // 2
        for side in range(2):
            halves[side].append(ref[0, which, side * rows : (side + 1) * rows, :])
    return jnp.concatenate(halves[0] + halves[1], 0)


def down_grad(grads, hiddens, chunk):
    experts, rows, width = grads[0].shape
    units = hiddens[0].shape[3]

    def kernel(own_ref, other_ref, *refs):
        hidden_refs, out_ref, active_ref = refs[:-2], refs[-2], refs[-1]

        @pl.when(pl.program_id(1) == 0)
        def _():
            gate, up = hidden_of(hidden_refs, 0), hidden_of(hidden_refs, 1)
            active_ref[...] = (gate * jax.nn.sigmoid(gate) * up).astype(jnp.bfloat16)

        block = jnp.concatenate([own_ref[0], other_ref[0]], 0)
        out_ref[0] = t_dot(active_ref[...], block).astype(jnp.bfloat16)

    row_block = pl.BlockSpec((1, rows, chunk), lambda e, s: (e, 0, s))
    return call(
        kernel,
        (experts, width // chunk),
        (*grads, *hiddens),
        [row_block, row_block]
        + [pl.BlockSpec((1,) + h.shape[1:], lambda e, s: (e, 0, 0, 0)) for h in hiddens],
        [shape((experts, units, width))],
        [pl.BlockSpec((1, units, chunk), lambda e, s: (e, 0, s))],
        4 * experts * rows * units * width,
        [pltpu.VMEM((2 * rows, units), jnp.bfloat16)],
        told=True,
    )[0]


def up_grads(back, groups, hiddens, chunk):
    experts, rows, units = back.shape
    width = groups[0][0].shape[2]
    count = len(groups)

    def kernel(back_ref, *refs):
        row_refs, hidden_refs = refs[: 2 * count], refs[2 * count : 3 * count]
        dg_ref, du_ref, dgate, dup = refs[3 * count :]

        @pl.when(pl.program_id(1) == 0)
        def _():
            gate, up = hidden_of(hidden_refs, 0), hidden_of(hidden_refs, 1)
            sig = jax.nn.sigmoid(gate)
            d_act = back_ref[0]
            dgate[...] = (d_act * up * sig * (1.0 + gate * (1.0 - sig))).astype(jnp.bfloat16)
            dup[...] = (d_act * (gate * sig)).astype(jnp.bfloat16)

        block = jnp.concatenate([ref[0] for ref in row_refs], 0)
        dg_ref[0] = t_dot(dgate[...], block).astype(jnp.bfloat16)
        du_ref[0] = t_dot(dup[...], block).astype(jnp.bfloat16)

    ordered = [group[side] for side in range(2) for group in groups]
    out_block = pl.BlockSpec((1, units, chunk), lambda e, s: (e, 0, s))
    return call(
        kernel,
        (experts, width // chunk),
        (back, *ordered, *hiddens),
        [pl.BlockSpec((1, rows, units), lambda e, s: (e, 0, 0))]
        + [pl.BlockSpec((1, o.shape[1], chunk), lambda e, s: (e, 0, s)) for o in ordered]
        + [pl.BlockSpec((1,) + h.shape[1:], lambda e, s: (e, 0, 0, 0)) for h in hiddens],
        [shape((experts, units, width))] * 2,
        [out_block] * 2,
        4 * experts * rows * units * width,
        [pltpu.VMEM((rows, units), jnp.bfloat16)] * 2,
        told=True,
    )


def attend(base, queries, pairs, out_proj):
    rows, width = queries.shape[0], out_proj.shape[1]
    tokens = pairs.shape[0]
    steps = queries.shape[1] // (2 * HEAD)

    def kernel(base_ref, query_ref, pairs_ref, proj_ref, out_ref, sum_ref):
        both = query_ref[...]
        query = jnp.concatenate([both[:, :HEAD], both[:, HEAD:]], 0)
        pairs = pairs_ref[...]
        scores = dot_t(query, pairs[:, :HEAD]) * (1.0 / math.sqrt(HEAD))
        query_pos = lax.broadcasted_iota(jnp.int32, (2 * rows, 1), 0) % rows + base_ref[0]
        key_pos = lax.broadcasted_iota(jnp.int32, (1, tokens), 1)
        scores = jnp.where(key_pos <= query_pos, scores, -1e30)
        probs = jnp.exp(scores - jnp.max(scores, axis=1, keepdims=True))
        denom = jnp.sum(probs, axis=1, keepdims=True)
        heads = jnp.dot(
            probs.astype(jnp.bfloat16), pairs[:, HEAD:], preferred_element_type=jnp.float32
        )
        heads = (heads / denom).astype(jnp.bfloat16)
        attn = jnp.concatenate([heads[:rows], heads[rows:]], 1)
        part = jnp.dot(attn, proj_ref[...], preferred_element_type=jnp.float32)
        step = pl.program_id(0)

        @pl.when(step == 0)
        def _():
            sum_ref[...] = part

        @pl.when(step > 0)
        def _():
            sum_ref[...] += part

        @pl.when(step == steps - 1)
        def _():
            out_ref[...] = sum_ref[...].astype(jnp.bfloat16)

    return call(
        kernel,
        (steps,),
        (base, queries, pairs, out_proj),
        [
            pl.BlockSpec(memory_space=pltpu.SMEM),
            pl.BlockSpec((rows, 2 * HEAD), lambda h: (0, h)),
            pl.BlockSpec((tokens, 2 * HEAD), lambda h: (0, 0)),
            pl.BlockSpec((2 * HEAD, width), lambda h: (h, 0)),
        ],
        [shape((rows, width))],
        [pl.BlockSpec((rows, width), lambda h: (0, 0))],
        2 * rows * queries.shape[1] * (2 * tokens + width),
        [pltpu.VMEM((rows, width), jnp.float32)],
        limit=32,
    )[0]


def shards(
    queries,
    keys,
    values,
    resid,
    out_proj,
    norm_gain,
    expert_ids,
    gates,
    w_gate,
    w_up,
    w_down,
    cotangent,
):
    width = resid.shape[1]
    chunk = min(512, width)
    yh, z, k, yl = (lax.axis_index(name) for name in ("yh", "z", "k", "yl"))
    ctx = ((yh * 4 + z) * 2 + k).astype(jnp.int32)

    tok_ctx = queries.shape[0]
    key_mine = lax.dynamic_slice_in_dim(keys, yl * HEAD, HEAD, 1)
    value_mine = lax.dynamic_slice_in_dim(values, yl * HEAD, HEAD, 1)
    pair = jnp.concatenate([key_mine, value_mine], 1)
    pairs = lax.all_to_all(
        jnp.broadcast_to(pair, (16,) + pair.shape), ("yh", "z", "k"), 0, 0, tiled=True
    ).reshape(16 * tok_ctx, 2 * HEAD)

    rest = gates
    pieces = [expert_ids.astype(jnp.bfloat16)]
    for _ in range(3):
        piece = lax.reduce_precision(rest, 8, 7)
        pieces.append(piece.astype(jnp.bfloat16))
        rest = rest - piece
    pieces.append(jnp.zeros((ROWS, META - 4 * TOPK), jnp.bfloat16))
    meta = jnp.concatenate(pieces, 1)
    cot_near = jnp.concatenate(gather_step(cotangent, stage_dims(0)), 0)
    cot_near = jnp.concatenate(gather_step(after(cot_near, pairs), stage_dims(1)), 0)
    cot_sides = gather_sides(cot_near)

    base = (ctx * tok_ctx).reshape(1)
    mixed = attend(base, queries, pairs, out_proj)
    mixed = lax.all_to_all(mixed, ("yl", "x"), 0, 0, tiled=True).reshape(8, ROWS, width)
    stream = resid.astype(jnp.float32) + jnp.sum(mixed.astype(jnp.float32), axis=0)
    normed = (
        stream * lax.rsqrt(jnp.mean(stream * stream, axis=1, keepdims=True) + 1e-06) * norm_gain
    ).astype(jnp.bfloat16)

    me = ctx.reshape(1)
    near = jnp.concatenate(
        gather_step(jnp.concatenate([normed, meta], 1), stage_dims(0)), 0
    )
    near = jnp.concatenate(gather_step(after(near, *cot_sides), stage_dims(1)), 0)
    left, right = gather_sides(near)
    half = near.shape[0] // 2
    narrow, wide = 2 * chunk, 4 * chunk

    def run_forward(rows_own, rows_got):
        return forward(rows_own, rows_got, w_gate, w_up, w_down, wide)

    own0, other0, place0, weight0 = pack_rows(me, [[near]], width, narrow)
    got0 = swap_cores(other0)
    out0, back0, hidden0 = run_forward(own0, got0)
    back0 = swap_cores(back0)
    left, right = after(left, out0), after(right, out0)

    far_a, far_b = gather_far(left, right)
    own1, other1, place1, weight1 = pack_rows(me, [[left], [right]], width, narrow)
    got1 = swap_cores(other1)
    (sum0,) = merge(place0, weight0, after(out0, other1), back0, [(2 * half, 2 * half, 0)], narrow)
    out1, back1, hidden1 = run_forward(after(own1, sum0), got1)
    back1 = swap_cores(back1)

    far_got = far_a
    far_a, far_b = after(far_a, out1), after(far_b, out1)
    own2, other2, place2, weight2 = pack_rows(me, [[far_a, far_b]], width, narrow)
    got2 = swap_cores(other2)
    out2, back2, hidden2 = run_forward(own2, got2)
    back2 = swap_cores(back2)

    dims = stage_dims(2)
    left_a, minus, plus, right_b = merge(
        place1,
        weight1,
        after(out1, out2),
        back1,
        [(half, half, 0), (half, 2 * half, 1), (half, 2 * half, 0), (half, half, 0)],
        narrow,
    )
    minus, plus = merge(
        place2,
        weight2,
        after(out2, left_a),
        back2,
        [(half, 2 * half, 0), (half, 2 * half, 1)],
        narrow,
        (minus, plus),
    )
    got_minus, got_plus = send(minus, dims, -1), send(plus, dims, 1)

    cot_left, cot_right = (after(side, far_got) for side in cot_sides)
    cot_far = gather_far(cot_left, cot_right)
    cot_tiles = [[after(cot_near, minus)], [cot_left], [cot_right], list(cot_far)]
    places, weights = (place0, place1, place2), (weight0, weight1, weight2)
    grads_own, grads_other = pack_grads(places, weights, cot_tiles, chunk)
    grads = (grads_own, swap_cores(grads_other))
    hiddens = [hidden0, hidden1, hidden2]

    left_a = add(after(left_a, grads_other), got_minus[:half]).astype(jnp.bfloat16)
    right_b = add(after(right_b, grads_other), got_plus[half:]).astype(jnp.bfloat16)
    got_left_a, got_right_b = send(left_a, dims, -1), send(right_b, dims, 1)
    back = back_act(grads, w_down, wide)
    sum0 = after(sum0, back)
    total = jnp.concatenate(
        [
            add(sum0[:half], got_left_a, got_plus[:half]),
            add(sum0[half:], got_minus[half:], got_right_b),
        ],
        0,
    )
    groups = [(own0, got0), (own1, got1), (own2, got2)]
    grad_down = down_grad(after_all(grads, back), hiddens, narrow)
    grad_gate, grad_up = up_grads(back, groups, hiddens, narrow)
    combined = scatter_near(total)
    layer_out = (stream + combined).astype(jnp.bfloat16)
    return layer_out, grad_gate, grad_up, grad_down


def solution(mesh):
    split = Mesh(mesh.devices.reshape(SIZES), AXES)
    ctx, tp = ("yh", "z", "k"), ("yl", "x")
    rows, weights = P(ctx + tp, None), P(ctx, tp, None)
    in_specs = (
        P(ctx, tp),
        P(ctx, None),
        P(ctx, None),
        rows,
        P(tp, None),
        P(),
        rows,
        rows,
        weights,
        weights,
        weights,
        rows,
    )
    return jax.shard_map(
        shards,
        mesh=split,
        in_specs=in_specs,
        out_specs=(rows, weights, weights, weights),
        check_vma=False,
    )
```

```python
import math

import jax
import jax.numpy as jnp
from jax import lax
from jax.experimental import pallas as pl
from jax.experimental.pallas import tpu as pltpu
from jax.sharding import Mesh
from jax.sharding import PartitionSpec as P

QHEADS = 32
KVHEADS = 2
HEAD = 128
TOPK = 8
CAP = 5
ROWS = 16
META = 128
SIZES = (2, 4, 2, 2, 4)
AXES = ("yh", "z", "k", "yl", "x")


def device_index(yh, z, k, yl, x):
    return (((yh * 4 + z) * 2 + k) * 2 + yl) * 4 + x


def shifted(dims, step):
    pairs = []
    for x in range(4):
        for y in range(4):
            for z in range(4):
                for k in range(2):
                    at = {"x": x, "y": y, "z": z}
                    to = dict(at)
                    to[dims[k]] = (to[dims[k]] + step) % 4
                    pairs.append(
                        (
                            device_index(at["y"] // 2, at["z"], k, at["y"] % 2, at["x"]),
                            device_index(to["y"] // 2, to["z"], k, to["y"] % 2, to["x"]),
                        )
                    )
    return pairs


def send(array, dims, step):
    return lax.ppermute(array, AXES, shifted(dims, step))


def swap_cores(arrays):
    return [lax.ppermute(array, "k", [(0, 1), (1, 0)]) for array in arrays]


def gather_step(block, dims):
    return [block, send(block, dims, 1), send(block, dims, -1), send(block, dims, 2)]


ORDERS = ("xyz", "zxy")


def stage_dims(stage):
    return (ORDERS[0][stage], ORDERS[1][stage])


def after(array, *others):
    return lax.optimization_barrier((array,) + others)[0]


def after_all(arrays, *others):
    return tuple(after(array, *others) for array in arrays)


def gather_near(block):
    for stage in range(2):
        block = jnp.concatenate(gather_step(block, stage_dims(stage)), 0)
    return block


def gather_sides(block):
    dims = stage_dims(2)
    return send(block, dims, 1), send(block, dims, -1)


def gather_far(left, right):
    dims = stage_dims(2)
    half = left.shape[0] // 2
    return send(left[:half], dims, 1), send(right[half:], dims, -1)


def add(*terms):
    total = terms[0].astype(jnp.float32)
    for term in terms[1:]:
        total = total + term.astype(jnp.float32)
    return total


def scatter_near(total):
    for stage in (1, 0):
        dims = stage_dims(stage)
        parts = total.astype(jnp.bfloat16).reshape(4, -1, total.shape[1])
        total = add(
            parts[0], send(parts[1], dims, -1), send(parts[2], dims, 1), send(parts[3], dims, -2)
        )
    return total


def placement(meta, experts, me):
    rows = meta.shape[0]
    slots = rows // ROWS * CAP
    turned = meta.astype(jnp.float32).T
    ids = turned[0:TOPK]
    gates = turned[TOPK : 2 * TOPK] + turned[2 * TOPK : 3 * TOPK] + turned[3 * TOPK : 4 * TOPK]
    token = lax.broadcasted_iota(jnp.int32, (rows, rows), 0)
    later = lax.broadcasted_iota(jnp.int32, (rows, rows), 1)
    earlier = ((token // ROWS == later // ROWS) & (token < later)).astype(jnp.float32)
    block = (lax.broadcasted_iota(jnp.int32, (1, rows), 1) // ROWS).astype(jnp.float32)
    slot_at = lax.broadcasted_iota(jnp.int32, (slots, rows), 0).astype(jnp.float32)
    places, weights = [], []
    for side in range(2):
        for local in range(experts):
            expert = ((me ^ side) * experts + local).astype(jnp.float32)
            named = ids == expert
            hit = jnp.max(named.astype(jnp.float32), axis=0, keepdims=True)
            gate = jnp.sum(jnp.where(named, gates, 0.0), axis=0, keepdims=True)
            rank = jnp.dot(
                jnp.broadcast_to(hit, (8, rows)), earlier, preferred_element_type=jnp.float32
            )[0:1]
            slot = jnp.where(hit > 0.0, block * CAP + rank, -1.0)
            place = (slot_at == slot).astype(jnp.float32)
            places.append(place)
            weights.append(jnp.sum(place * gate, axis=1, keepdims=True))
    return jnp.concatenate(places, 0), jnp.concatenate(weights, 0)


def cost(flops, *arrays):
    moved = sum(array.size * array.dtype.itemsize for array in arrays)
    return pl.CostEstimate(flops=int(flops), bytes_accessed=int(moved), transcendentals=0)


def call(kernel, grid, ins, in_specs, outs, out_specs, flops, scratch=(), limit=24, told=False):
    return pl.pallas_call(
        kernel,
        grid=grid,
        in_specs=in_specs,
        out_specs=out_specs,
        out_shape=outs,
        scratch_shapes=list(scratch),
        compiler_params=pltpu.CompilerParams(vmem_limit_bytes=limit * 1024 * 1024),
        cost_estimate=cost(flops, *ins, *outs) if told else None,
    )(*ins)


def shape(dims, dtype=jnp.bfloat16):
    return jax.ShapeDtypeStruct(dims, dtype)


def joined(refs):
    return refs[0][...] if len(refs) == 1 else jnp.concatenate([ref[...] for ref in refs], 0)


def store_slots(found, own_ref, other_refs):
    slots = found[0].shape[0] // 4
    for e in range(2):
        own_ref[e] = jnp.concatenate([tile[e * slots : (e + 1) * slots] for tile in found], 0)
        rows = jnp.concatenate([tile[(e + 2) * slots : (e + 3) * slots] for tile in found], 0)
        at = 0
        for ref in other_refs:
            ref[e] = rows[at : at + ref.shape[1]]
            at += ref.shape[1]


def pack_rows(me, groups, cuts, width, chunk):
    parts = [part for group in groups for part in group]
    tile_rows = sum(part.shape[0] for part in groups[0])
    slots = tile_rows // ROWS * CAP
    count, total = len(groups), len(parts)
    meta_at = width // META

    def kernel(me_ref, *refs):
        metas, rows = refs[:total], refs[total : 2 * total]
        own_ref, *other_refs, place_ref, weight_ref = refs[2 * total :]

        @pl.when(pl.program_id(0) == 0)
        def _():
            at = 0
            for tile, group in enumerate(groups):
                meta = joined(metas[at : at + len(group)])
                at += len(group)
                place, weight = placement(meta, 2, me_ref[0])
                place_ref[tile] = place.astype(jnp.bfloat16)
                weight_ref[tile] = jnp.broadcast_to(weight, weight_ref.shape[1:])

        at, found = 0, []
        for tile, group in enumerate(groups):
            block = joined(rows[at : at + len(group)])
            at += len(group)
            rows_of = jnp.dot(place_ref[tile], block, preferred_element_type=jnp.float32)
            found.append(rows_of.astype(jnp.bfloat16))
        store_slots(found, own_ref, other_refs)

    own, *others, place, weight = call(
        kernel,
        (width // chunk,),
        (me, *parts, *parts),
        [pl.BlockSpec(memory_space=pltpu.SMEM)]
        + [pl.BlockSpec((part.shape[0], META), lambda j: (0, meta_at)) for part in parts]
        + [pl.BlockSpec((part.shape[0], chunk), lambda j: (0, j)) for part in parts],
        [shape((2, count * slots, width))]
        + [shape((2, cut, width)) for cut in cuts]
        + [
            shape((count, 4 * slots, tile_rows)),
            shape((count, 4 * slots, META), jnp.float32),
        ],
        [pl.BlockSpec((2, count * slots, chunk), lambda j: (0, 0, j))]
        + [pl.BlockSpec((2, cut, chunk), lambda j: (0, 0, j)) for cut in cuts]
        + [
            pl.BlockSpec((count, 4 * slots, tile_rows), lambda j: (0, 0, 0)),
            pl.BlockSpec((count, 4 * slots, META), lambda j: (0, 0, 0)),
        ],
        2 * count * 4 * slots * tile_rows * width,
    )
    return own, others, place, weight


def pack_grads(places, weights, tiles, chunk):
    parts = [part for group in tiles for part in group]
    width = parts[0].shape[1]
    tile_rows = places[0].shape[2]
    slots = places[0].shape[1] // 4
    count = len(places)

    def kernel(*refs):
        place_refs, weight_refs = refs[:count], refs[count : 2 * count]
        rows = refs[2 * count : 2 * count + len(parts)]
        own_ref, *other_refs = refs[2 * count + len(parts) :]
        placed = [ref[t] for ref in place_refs for t in range(ref.shape[0])]
        scales = [ref[t] for ref in weight_refs for t in range(ref.shape[0])]
        at, found = 0, []
        for tile, group in enumerate(tiles):
            block = joined(rows[at : at + len(group)])
            at += len(group)
            rows_of = jnp.dot(placed[tile], block, preferred_element_type=jnp.float32)
            found.append((rows_of * scales[tile][:, 0:1]).astype(jnp.bfloat16))
        store_slots(found, own_ref, other_refs)

    own, *others = call(
        kernel,
        (width // chunk,),
        (*places, *weights, *parts),
        [pl.BlockSpec(a.shape, lambda j: (0, 0, 0)) for a in (*places, *weights)]
        + [pl.BlockSpec((part.shape[0], chunk), lambda j: (0, j)) for part in parts],
        [shape((2, len(tiles) * slots, width))] + [shape((2, slots, width))] * len(tiles),
        [pl.BlockSpec((2, len(tiles) * slots, chunk), lambda j: (0, 0, j))]
        + [pl.BlockSpec((2, slots, chunk), lambda j: (0, 0, j))] * len(tiles),
        2 * len(tiles) * 4 * slots * tile_rows * width,
        told=True,
    )
    return own, others


def merge(place, weight, own, others, pieces, chunk, into=()):
    width = own.shape[2]
    rows = place.shape[2]
    slots = place.shape[1] // 4
    count = own.shape[1] // slots

    def kernel(place_ref, weight_ref, own_ref, *refs):
        outs = refs[len(others) + len(into) :]
        other_rows = [
            jnp.concatenate([ref[e] for ref in refs[: len(others)]], 0) for e in range(2)
        ]
        totals = []
        for tile in range(count):
            span = pl.ds(tile * slots, slots)
            block = jnp.concatenate(
                [own_ref[e, span, :] for e in range(2)]
                + [rows_of[tile * slots : (tile + 1) * slots] for rows_of in other_rows],
                0,
            )
            scale = weight_ref[tile][:, 0:1]
            scaled = (block.astype(jnp.float32) * scale).astype(jnp.bfloat16)
            totals.append(t_dot(place_ref[tile], scaled).astype(jnp.bfloat16))
        at = 0
        for out, (size, _, _) in zip(outs, pieces):
            out[...] = totals[at // rows][at % rows : at % rows + size]
            at += size

    return pl.pallas_call(
        kernel,
        grid=(width // chunk,),
        in_specs=[
            pl.BlockSpec(place.shape, lambda j: (0, 0, 0)),
            pl.BlockSpec(weight.shape, lambda j: (0, 0, 0)),
            pl.BlockSpec((2, own.shape[1], chunk), lambda j: (0, 0, j)),
        ]
        + [pl.BlockSpec((2, other.shape[1], chunk), lambda j: (0, 0, j)) for other in others]
        + [pl.BlockSpec(memory_space=pl.ANY)] * len(into),
        out_specs=[
            pl.BlockSpec((size, chunk), lambda j, at=at: (at, j)) for size, _, at in pieces
        ],
        out_shape=[shape((total, width)) for _, total, _ in pieces],
        input_output_aliases={3 + len(others) + i: i for i in range(len(into))},
        compiler_params=pltpu.CompilerParams(vmem_limit_bytes=24 * 1024 * 1024),
    )(place, weight, own, *others, *into)


def dot_t(a, b):
    return lax.dot_general(a, b, (((1,), (1,)), ((), ())), preferred_element_type=jnp.float32)


def t_dot(a, b):
    return lax.dot_general(a, b, (((0,), (0,)), ((), ())), preferred_element_type=jnp.float32)


def forward(own, others, backs_cuts, w_gate, w_up, w_down, chunk):
    experts, rows, width = own.shape
    hidden = w_gate.shape[1]
    steps = width // chunk
    count = len(others)

    def kernel(own_ref, *refs):
        other_refs, (wg_ref, wu_ref, wd_ref) = refs[:count], refs[count : count + 3]
        own_out, *other_outs, hidden_ref, gate_sum, up_sum, active_ref = refs[count + 3 :]
        step = pl.program_id(1)

        @pl.when(step < steps)
        def _():
            block = jnp.concatenate([own_ref[0]] + [ref[0] for ref in other_refs], 0)
            gate = dot_t(block, wg_ref[0])
            up = dot_t(block, wu_ref[0])

            @pl.when(step == 0)
            def _():
                gate_sum[...] = gate
                up_sum[...] = up

            @pl.when(step > 0)
            def _():
                gate_sum[...] += gate
                up_sum[...] += up

        @pl.when(step == steps)
        def _():
            gate, up = gate_sum[...], up_sum[...]
            hidden_ref[0, 0] = gate
            hidden_ref[0, 1] = up
            active_ref[...] = (gate * jax.nn.sigmoid(gate) * up).astype(jnp.bfloat16)

        @pl.when(step >= steps)
        def _():
            out = jnp.dot(active_ref[...], wd_ref[0], preferred_element_type=jnp.float32)
            out = out.astype(jnp.bfloat16)
            own_out[0] = out[:rows]
            at = rows
            for other_out in other_outs:
                other_out[0] = out[at : at + other_out.shape[1]]
                at += other_out.shape[1]

    def early(e, s):
        return (e, 0, jnp.minimum(s, steps - 1))

    def late(e, s):
        return (e, 0, jnp.maximum(s - steps, 0))

    row_block = pl.BlockSpec((1, rows, chunk), early)
    weight_block = pl.BlockSpec((1, hidden, chunk), early)
    out, *backs, values = call(
        kernel,
        (experts, 2 * steps),
        (own, *others, w_gate, w_up, w_down),
        [row_block]
        + [pl.BlockSpec((1, other.shape[1], chunk), early) for other in others]
        + [weight_block, weight_block, pl.BlockSpec((1, hidden, chunk), late)],
        [shape(own.shape)] + [shape((experts, cut, width)) for cut in backs_cuts]
        + [shape((experts, 2, 2 * rows, hidden), jnp.float32)],
        [
            pl.BlockSpec((1, rows, chunk), late),
            *[pl.BlockSpec((1, cut, chunk), late) for cut in backs_cuts],
            pl.BlockSpec((1, 2, 2 * rows, hidden), lambda e, s: (e, 0, 0, 0)),
        ],
        12 * experts * rows * hidden * width,
        [
            pltpu.VMEM((2 * rows, hidden), jnp.float32),
            pltpu.VMEM((2 * rows, hidden), jnp.float32),
            pltpu.VMEM((2 * rows, hidden), jnp.bfloat16),
        ],
    )
    return out, backs, values


def back_act(grads, w_down, chunk):
    experts, _, width = grads[0].shape
    rows = sum(part.shape[1] for part in grads)
    hidden = w_down.shape[1]

    def kernel(*refs):
        wd_ref, out_ref = refs[-2:]
        found = dot_t(jnp.concatenate([ref[0] for ref in refs[:-2]], 0), wd_ref[0])

        @pl.when(pl.program_id(1) == 0)
        def _():
            out_ref[0] = found

        @pl.when(pl.program_id(1) > 0)
        def _():
            out_ref[0] += found

    return call(
        kernel,
        (experts, width // chunk),
        (*grads, w_down),
        [pl.BlockSpec((1, part.shape[1], chunk), lambda e, s: (e, 0, s)) for part in grads]
        + [pl.BlockSpec((1, hidden, chunk), lambda e, s: (e, 0, s))],
        [shape((experts, rows, hidden), jnp.float32)],
        [pl.BlockSpec((1, rows, hidden), lambda e, s: (e, 0, 0))],
        2 * experts * rows * hidden * width,
        told=True,
    )[0]


def hidden_of(refs, which):
    halves = [[], []]
    for ref in refs:
        rows = ref.shape[2] // 2
        for side in range(2):
            halves[side].append(ref[0, which, side * rows : (side + 1) * rows, :])
    return jnp.concatenate(halves[0] + halves[1], 0)


def down_grad(grads, hiddens, chunk):
    experts, _, width = grads[0].shape
    rows = sum(part.shape[1] for part in grads)
    units = hiddens[0].shape[3]
    count = len(grads)

    def kernel(*refs):
        hidden_refs, out_ref, active_ref = refs[count:-2], refs[-2], refs[-1]

        @pl.when(pl.program_id(1) == 0)
        def _():
            gate, up = hidden_of(hidden_refs, 0), hidden_of(hidden_refs, 1)
            active_ref[...] = (gate * jax.nn.sigmoid(gate) * up).astype(jnp.bfloat16)

        block = jnp.concatenate([ref[0] for ref in refs[:count]], 0)
        out_ref[0] = t_dot(active_ref[...], block).astype(jnp.bfloat16)

    return call(
        kernel,
        (experts, width // chunk),
        (*grads, *hiddens),
        [pl.BlockSpec((1, part.shape[1], chunk), lambda e, s: (e, 0, s)) for part in grads]
        + [pl.BlockSpec((1,) + h.shape[1:], lambda e, s: (e, 0, 0, 0)) for h in hiddens],
        [shape((experts, units, width))],
        [pl.BlockSpec((1, units, chunk), lambda e, s: (e, 0, s))],
        2 * experts * rows * units * width,
        [pltpu.VMEM((rows, units), jnp.bfloat16)],
        told=True,
    )[0]


def up_grads(back, ordered, hiddens, chunk):
    experts, rows, units = back.shape
    width = ordered[0].shape[2]
    count = len(ordered)

    def kernel(back_ref, *refs):
        row_refs, hidden_refs = refs[:count], refs[count:-4]
        dg_ref, du_ref, dgate, dup = refs[-4:]

        @pl.when(pl.program_id(1) == 0)
        def _():
            gate, up = hidden_of(hidden_refs, 0), hidden_of(hidden_refs, 1)
            sig = jax.nn.sigmoid(gate)
            d_act = back_ref[0]
            dgate[...] = (d_act * up * sig * (1.0 + gate * (1.0 - sig))).astype(jnp.bfloat16)
            dup[...] = (d_act * (gate * sig)).astype(jnp.bfloat16)

        block = jnp.concatenate([ref[0] for ref in row_refs], 0)
        dg_ref[0] = t_dot(dgate[...], block).astype(jnp.bfloat16)
        du_ref[0] = t_dot(dup[...], block).astype(jnp.bfloat16)

    out_block = pl.BlockSpec((1, units, chunk), lambda e, s: (e, 0, s))
    return call(
        kernel,
        (experts, width // chunk),
        (back, *ordered, *hiddens),
        [pl.BlockSpec((1, rows, units), lambda e, s: (e, 0, 0))]
        + [pl.BlockSpec((1, o.shape[1], chunk), lambda e, s: (e, 0, s)) for o in ordered]
        + [pl.BlockSpec((1,) + h.shape[1:], lambda e, s: (e, 0, 0, 0)) for h in hiddens],
        [shape((experts, units, width))] * 2,
        [out_block] * 2,
        4 * experts * rows * units * width,
        [pltpu.VMEM((rows, units), jnp.bfloat16)] * 2,
        told=True,
    )


def attend(base, queries, pairs, out_proj):
    rows, width = queries.shape[0], out_proj.shape[1]
    tokens = pairs.shape[0]
    steps = queries.shape[1] // (2 * HEAD)

    def kernel(base_ref, query_ref, pairs_ref, proj_ref, out_ref, sum_ref):
        both = query_ref[...]
        query = jnp.concatenate([both[:, :HEAD], both[:, HEAD:]], 0)
        pairs = pairs_ref[...]
        scores = dot_t(query, pairs[:, :HEAD]) * (1.0 / math.sqrt(HEAD))
        query_pos = lax.broadcasted_iota(jnp.int32, (2 * rows, 1), 0) % rows + base_ref[0]
        key_pos = lax.broadcasted_iota(jnp.int32, (1, tokens), 1)
        scores = jnp.where(key_pos <= query_pos, scores, -1e30)
        probs = jnp.exp(scores - jnp.max(scores, axis=1, keepdims=True))
        denom = jnp.sum(probs, axis=1, keepdims=True)
        heads = jnp.dot(
            probs.astype(jnp.bfloat16), pairs[:, HEAD:], preferred_element_type=jnp.float32
        )
        heads = (heads / denom).astype(jnp.bfloat16)
        attn = jnp.concatenate([heads[:rows], heads[rows:]], 1)
        part = jnp.dot(attn, proj_ref[...], preferred_element_type=jnp.float32)
        step = pl.program_id(0)

        @pl.when(step == 0)
        def _():
            sum_ref[...] = part

        @pl.when(step > 0)
        def _():
            sum_ref[...] += part

        @pl.when(step == steps - 1)
        def _():
            out_ref[...] = sum_ref[...].astype(jnp.bfloat16)

    return call(
        kernel,
        (steps,),
        (base, queries, pairs, out_proj),
        [
            pl.BlockSpec(memory_space=pltpu.SMEM),
            pl.BlockSpec((rows, 2 * HEAD), lambda h: (0, h)),
            pl.BlockSpec((tokens, 2 * HEAD), lambda h: (0, 0)),
            pl.BlockSpec((2 * HEAD, width), lambda h: (h, 0)),
        ],
        [shape((rows, width))],
        [pl.BlockSpec((rows, width), lambda h: (0, 0))],
        2 * rows * queries.shape[1] * (2 * tokens + width),
        [pltpu.VMEM((rows, width), jnp.float32)],
        limit=56,
    )[0]


def shards(
    queries,
    keys,
    values,
    resid,
    out_proj,
    norm_gain,
    expert_ids,
    gates,
    w_gate,
    w_up,
    w_down,
    cotangent,
):
    width = resid.shape[1]
    chunk = min(512, width)
    yh, z, k, yl = (lax.axis_index(name) for name in ("yh", "z", "k", "yl"))
    ctx = ((yh * 4 + z) * 2 + k).astype(jnp.int32)

    tok_ctx = queries.shape[0]
    key_mine = lax.dynamic_slice_in_dim(keys, yl * HEAD, HEAD, 1)
    value_mine = lax.dynamic_slice_in_dim(values, yl * HEAD, HEAD, 1)
    pair = jnp.concatenate([key_mine, value_mine], 1)
    pairs = lax.all_to_all(
        jnp.broadcast_to(pair, (16,) + pair.shape), ("yh", "z", "k"), 0, 0, tiled=True
    ).reshape(16 * tok_ctx, 2 * HEAD)

    rest = gates
    pieces = [expert_ids.astype(jnp.bfloat16)]
    for _ in range(3):
        piece = lax.reduce_precision(rest, 8, 7)
        pieces.append(piece.astype(jnp.bfloat16))
        rest = rest - piece
    pieces.append(jnp.zeros((ROWS, META - 4 * TOPK), jnp.bfloat16))
    meta = jnp.concatenate(pieces, 1)
    cot_near = jnp.concatenate(gather_step(cotangent, stage_dims(0)), 0)
    cot_near = jnp.concatenate(gather_step(after(cot_near, pairs), stage_dims(1)), 0)
    cot_sides = gather_sides(cot_near)

    base = (ctx * tok_ctx).reshape(1)
    mixed = attend(base, queries, pairs, out_proj)
    mixed = lax.all_to_all(mixed, ("yl", "x"), 0, 0, tiled=True).reshape(8, ROWS, width)
    stream = resid.astype(jnp.float32) + jnp.sum(mixed.astype(jnp.float32), axis=0)
    normed = (
        stream * lax.rsqrt(jnp.mean(stream * stream, axis=1, keepdims=True) + 1e-06) * norm_gain
    ).astype(jnp.bfloat16)

    me = ctx.reshape(1)
    near = jnp.concatenate(
        gather_step(jnp.concatenate([normed, meta], 1), stage_dims(0)), 0
    )
    near = after(jnp.concatenate(gather_step(near, stage_dims(1)), 0), *cot_sides)
    left, right = gather_sides(near)
    half = near.shape[0] // 2
    narrow, wide = 2 * chunk, 4 * chunk

    slots = near.shape[0] // ROWS * CAP
    cuts = [slots // 32 * 16 + 16, slots // 32 * 16]
    thirds = [cuts[0], 2 * cuts[1], cuts[0]]

    def run_forward(rows_own, rows_got, backs):
        return forward(rows_own, rows_got, backs, w_gate, w_up, w_down, wide)

    own0, other0, place0, weight0 = pack_rows(me, [[near]], [slots], width, narrow)
    got0 = swap_cores(other0)
    out0, back0, hidden0 = run_forward(own0, got0, [slots])
    back0 = swap_cores(back0)
    left, right = after(left, out0), after(right, out0)

    far_a, far_b = gather_far(left, right)
    own1, other1, place1, weight1 = pack_rows(me, [[left], [right]], thirds, width, narrow)
    got1 = swap_cores(other1)
    (sum0,) = merge(place0, weight0, after(out0, *other1), back0, [(2 * half, 2 * half, 0)], narrow)
    out1, back1, hidden1 = run_forward(after(own1, sum0), got1, [2 * slots])
    back1 = swap_cores(back1)

    cot_left, cot_right = (after(side, far_a) for side in cot_sides)
    cot_far = gather_far(cot_left, cot_right)
    far_a, far_b = after(far_a, out1), after(far_b, out1)
    own2, other2, place2, weight2 = pack_rows(me, [[far_a, far_b]], cuts, width, narrow)
    got2 = swap_cores(other2)
    out2, back2, hidden2 = run_forward(own2, got2, cuts)
    back2 = swap_cores(back2)

    dims = stage_dims(2)
    left_a, minus, plus, right_b = merge(
        place1,
        weight1,
        after(out1, out2),
        back1,
        [(half, half, 0), (half, 2 * half, 1), (half, 2 * half, 0), (half, half, 0)],
        narrow,
    )
    minus, plus = merge(
        place2,
        weight2,
        after(out2, left_a, *cot_far),
        back2,
        [(half, 2 * half, 0), (half, 2 * half, 1)],
        narrow,
        (minus, plus),
    )
    got_minus, got_plus = send(minus, dims, -1), send(plus, dims, 1)

    cot_tiles = [[cot_near], [cot_left], [cot_right], list(cot_far)]
    places, weights = (place0, place1, place2), (weight0, weight1, weight2)
    grads_own, grads_other = pack_grads(places, weights, cot_tiles, chunk)
    grads = [grads_own] + swap_cores(grads_other)
    hiddens = [hidden0, hidden1, hidden2]

    left_a = add(left_a, got_minus[:half]).astype(jnp.bfloat16)
    right_b = add(right_b, got_plus[half:]).astype(jnp.bfloat16)
    got_left_a, got_right_b = send(left_a, dims, -1), send(right_b, dims, 1)
    back = back_act(grads, w_down, wide)
    sum0 = after(sum0, back)
    total = jnp.concatenate(
        [
            add(sum0[:half], got_left_a, got_plus[:half]),
            add(sum0[half:], got_minus[half:], got_right_b),
        ],
        0,
    )
    grad_down = down_grad(after_all(grads, back), hiddens, narrow)
    rows = [own0, own1, own2] + got0 + got1 + got2
    grad_gate, grad_up = up_grads(back, rows, hiddens, narrow)
    combined = scatter_near(total)
    layer_out = (stream + combined).astype(jnp.bfloat16)
    return layer_out, grad_gate, grad_up, grad_down


def solution(mesh):
    split = Mesh(mesh.devices.reshape(SIZES), AXES)
    ctx, tp = ("yh", "z", "k"), ("yl", "x")
    rows, weights = P(ctx + tp, None), P(ctx, tp, None)
    in_specs = (
        P(ctx, tp),
        P(ctx, None),
        P(ctx, None),
        rows,
        P(tp, None),
        P(),
        rows,
        rows,
        weights,
        weights,
        weights,
        rows,
    )
    return jax.shard_map(
        shards,
        mesh=split,
        in_specs=in_specs,
        out_specs=(rows, weights, weights, weights),
        check_vma=False,
    )
```

```python
import math

import jax
import jax.numpy as jnp
from jax import lax
from jax.experimental import pallas as pl
from jax.experimental.pallas import tpu as pltpu
from jax.sharding import Mesh
from jax.sharding import PartitionSpec as P

QHEADS = 32
KVHEADS = 2
HEAD = 128
TOPK = 8
CAP = 5
ROWS = 16
META = 128
SIZES = (2, 4, 2, 2, 4)
AXES = ("yh", "z", "k", "yl", "x")


def device_index(yh, z, k, yl, x):
    return (((yh * 4 + z) * 2 + k) * 2 + yl) * 4 + x


def shifted(dims, step):
    pairs = []
    for x in range(4):
        for y in range(4):
            for z in range(4):
                for k in range(2):
                    at = {"x": x, "y": y, "z": z}
                    to = dict(at)
                    to[dims[k]] = (to[dims[k]] + step) % 4
                    pairs.append(
                        (
                            device_index(at["y"] // 2, at["z"], k, at["y"] % 2, at["x"]),
                            device_index(to["y"] // 2, to["z"], k, to["y"] % 2, to["x"]),
                        )
                    )
    return pairs


def send(array, dims, step):
    return lax.ppermute(array, AXES, shifted(dims, step))


def swap_cores(arrays):
    return [lax.ppermute(array, "k", [(0, 1), (1, 0)]) for array in arrays]


def gather_step(block, dims):
    return [block, send(block, dims, 1), send(block, dims, -1), send(block, dims, 2)]


ORDERS = ("xyz", "zxy")


def stage_dims(stage):
    return (ORDERS[0][stage], ORDERS[1][stage])


def after(array, *others):
    return lax.optimization_barrier((array,) + others)[0]


def after_all(arrays, *others):
    return tuple(after(array, *others) for array in arrays)


def gather_near(block):
    for stage in range(2):
        block = jnp.concatenate(gather_step(block, stage_dims(stage)), 0)
    return block


def gather_sides(block):
    dims = stage_dims(2)
    return send(block, dims, 1), send(block, dims, -1)


def gather_far(left, right):
    dims = stage_dims(2)
    half = left.shape[0] // 2
    return send(left[:half], dims, 1), send(right[half:], dims, -1)


def add(*terms):
    total = terms[0].astype(jnp.float32)
    for term in terms[1:]:
        total = total + term.astype(jnp.float32)
    return total


def scatter_near(total):
    for stage in (1, 0):
        dims = stage_dims(stage)
        parts = total.astype(jnp.bfloat16).reshape(4, -1, total.shape[1])
        total = add(
            parts[0], send(parts[1], dims, -1), send(parts[2], dims, 1), send(parts[3], dims, -2)
        )
    return total


def placement(meta, experts, me):
    rows = meta.shape[0]
    slots = rows // ROWS * CAP
    turned = meta.astype(jnp.float32).T
    ids = turned[0:TOPK]
    gates = turned[TOPK : 2 * TOPK] + turned[2 * TOPK : 3 * TOPK] + turned[3 * TOPK : 4 * TOPK]
    token = lax.broadcasted_iota(jnp.int32, (rows, rows), 0)
    later = lax.broadcasted_iota(jnp.int32, (rows, rows), 1)
    earlier = ((token // ROWS == later // ROWS) & (token < later)).astype(jnp.float32)
    block = (lax.broadcasted_iota(jnp.int32, (1, rows), 1) // ROWS).astype(jnp.float32)
    slot_at = lax.broadcasted_iota(jnp.int32, (slots, rows), 0).astype(jnp.float32)
    places, weights = [], []
    for side in range(2):
        for local in range(experts):
            expert = ((me ^ side) * experts + local).astype(jnp.float32)
            named = ids == expert
            hit = jnp.max(named.astype(jnp.float32), axis=0, keepdims=True)
            gate = jnp.sum(jnp.where(named, gates, 0.0), axis=0, keepdims=True)
            rank = jnp.dot(
                jnp.broadcast_to(hit, (8, rows)), earlier, preferred_element_type=jnp.float32
            )[0:1]
            slot = jnp.where(hit > 0.0, block * CAP + rank, -1.0)
            place = (slot_at == slot).astype(jnp.float32)
            places.append(place)
            weights.append(jnp.sum(place * gate, axis=1, keepdims=True))
    return jnp.concatenate(places, 0), jnp.concatenate(weights, 0)


def cost(flops, *arrays):
    moved = sum(array.size * array.dtype.itemsize for array in arrays)
    return pl.CostEstimate(flops=int(flops), bytes_accessed=int(moved), transcendentals=0)


def call(kernel, grid, ins, in_specs, outs, out_specs, flops, scratch=(), limit=24, told=False):
    return pl.pallas_call(
        kernel,
        grid=grid,
        in_specs=in_specs,
        out_specs=out_specs,
        out_shape=outs,
        scratch_shapes=list(scratch),
        compiler_params=pltpu.CompilerParams(vmem_limit_bytes=limit * 1024 * 1024),
        cost_estimate=cost(flops, *ins, *outs) if told else None,
    )(*ins)


def shape(dims, dtype=jnp.bfloat16):
    return jax.ShapeDtypeStruct(dims, dtype)


def joined(refs):
    return refs[0][...] if len(refs) == 1 else jnp.concatenate([ref[...] for ref in refs], 0)


def store_slots(found, own_ref, other_refs):
    slots = found[0].shape[0] // 4
    for e in range(2):
        own_ref[e] = jnp.concatenate([tile[e * slots : (e + 1) * slots] for tile in found], 0)
        rows = jnp.concatenate([tile[(e + 2) * slots : (e + 3) * slots] for tile in found], 0)
        at = 0
        for ref in other_refs:
            ref[e] = rows[at : at + ref.shape[1]]
            at += ref.shape[1]


def pack_rows(me, groups, cuts, width, chunk):
    parts = [part for group in groups for part in group]
    tile_rows = sum(part.shape[0] for part in groups[0])
    slots = tile_rows // ROWS * CAP
    count, total = len(groups), len(parts)
    meta_at = width // META

    def kernel(me_ref, *refs):
        metas, rows = refs[:total], refs[total : 2 * total]
        own_ref, *other_refs, place_ref, weight_ref = refs[2 * total :]

        @pl.when(pl.program_id(0) == 0)
        def _():
            at = 0
            for tile, group in enumerate(groups):
                meta = joined(metas[at : at + len(group)])
                at += len(group)
                place, weight = placement(meta, 2, me_ref[0])
                place_ref[tile] = place.astype(jnp.bfloat16)
                weight_ref[tile] = jnp.broadcast_to(weight, weight_ref.shape[1:])

        at, found = 0, []
        for tile, group in enumerate(groups):
            block = joined(rows[at : at + len(group)])
            at += len(group)
            rows_of = jnp.dot(place_ref[tile], block, preferred_element_type=jnp.float32)
            found.append(rows_of.astype(jnp.bfloat16))
        store_slots(found, own_ref, other_refs)

    own, *others, place, weight = call(
        kernel,
        (width // chunk,),
        (me, *parts, *parts),
        [pl.BlockSpec(memory_space=pltpu.SMEM)]
        + [pl.BlockSpec((part.shape[0], META), lambda j: (0, meta_at)) for part in parts]
        + [pl.BlockSpec((part.shape[0], chunk), lambda j: (0, j)) for part in parts],
        [shape((2, count * slots, width))]
        + [shape((2, cut, width)) for cut in cuts]
        + [
            shape((count, 4 * slots, tile_rows)),
            shape((count, 4 * slots, META), jnp.float32),
        ],
        [pl.BlockSpec((2, count * slots, chunk), lambda j: (0, 0, j))]
        + [pl.BlockSpec((2, cut, chunk), lambda j: (0, 0, j)) for cut in cuts]
        + [
            pl.BlockSpec((count, 4 * slots, tile_rows), lambda j: (0, 0, 0)),
            pl.BlockSpec((count, 4 * slots, META), lambda j: (0, 0, 0)),
        ],
        2 * count * 4 * slots * tile_rows * width,
    )
    return own, others, place, weight


def pack_grads(places, weights, tiles, chunk):
    parts = [part for group in tiles for part in group]
    width = parts[0].shape[1]
    tile_rows = places[0].shape[2]
    slots = places[0].shape[1] // 4
    count = len(places)

    def kernel(*refs):
        place_refs, weight_refs = refs[:count], refs[count : 2 * count]
        rows = refs[2 * count : 2 * count + len(parts)]
        own_ref, *other_refs = refs[2 * count + len(parts) :]
        placed = [ref[t] for ref in place_refs for t in range(ref.shape[0])]
        scales = [ref[t] for ref in weight_refs for t in range(ref.shape[0])]
        at, found = 0, []
        for tile, group in enumerate(tiles):
            block = joined(rows[at : at + len(group)])
            at += len(group)
            rows_of = jnp.dot(placed[tile], block, preferred_element_type=jnp.float32)
            found.append((rows_of * scales[tile][:, 0:1]).astype(jnp.bfloat16))
        store_slots(found, own_ref, other_refs)

    own, *others = call(
        kernel,
        (width // chunk,),
        (*places, *weights, *parts),
        [pl.BlockSpec(a.shape, lambda j: (0, 0, 0)) for a in (*places, *weights)]
        + [pl.BlockSpec((part.shape[0], chunk), lambda j: (0, j)) for part in parts],
        [shape((2, len(tiles) * slots, width))] + [shape((2, slots, width))] * len(tiles),
        [pl.BlockSpec((2, len(tiles) * slots, chunk), lambda j: (0, 0, j))]
        + [pl.BlockSpec((2, slots, chunk), lambda j: (0, 0, j))] * len(tiles),
        2 * len(tiles) * 4 * slots * tile_rows * width,
        told=True,
    )
    return own, others


def merge(place, weight, own, others, pieces, chunk, into=()):
    width = own.shape[2]
    rows = place.shape[2]
    slots = place.shape[1] // 4
    count = own.shape[1] // slots

    def kernel(place_ref, weight_ref, own_ref, *refs):
        outs = refs[len(others) + len(into) :]
        other_rows = [
            jnp.concatenate([ref[e] for ref in refs[: len(others)]], 0) for e in range(2)
        ]
        totals = []
        for tile in range(count):
            span = pl.ds(tile * slots, slots)
            block = jnp.concatenate(
                [own_ref[e, span, :] for e in range(2)]
                + [rows_of[tile * slots : (tile + 1) * slots] for rows_of in other_rows],
                0,
            )
            scale = weight_ref[tile][:, 0:1]
            scaled = (block.astype(jnp.float32) * scale).astype(jnp.bfloat16)
            totals.append(t_dot(place_ref[tile], scaled).astype(jnp.bfloat16))
        at = 0
        for out, (size, _, _) in zip(outs, pieces):
            out[...] = totals[at // rows][at % rows : at % rows + size]
            at += size

    return pl.pallas_call(
        kernel,
        grid=(width // chunk,),
        in_specs=[
            pl.BlockSpec(place.shape, lambda j: (0, 0, 0)),
            pl.BlockSpec(weight.shape, lambda j: (0, 0, 0)),
            pl.BlockSpec((2, own.shape[1], chunk), lambda j: (0, 0, j)),
        ]
        + [pl.BlockSpec((2, other.shape[1], chunk), lambda j: (0, 0, j)) for other in others]
        + [pl.BlockSpec(memory_space=pl.ANY)] * len(into),
        out_specs=[
            pl.BlockSpec((size, chunk), lambda j, at=at: (at, j)) for size, _, at in pieces
        ],
        out_shape=[shape((total, width)) for _, total, _ in pieces],
        input_output_aliases={3 + len(others) + i: i for i in range(len(into))},
        compiler_params=pltpu.CompilerParams(vmem_limit_bytes=24 * 1024 * 1024),
    )(place, weight, own, *others, *into)


def dot_t(a, b):
    return lax.dot_general(a, b, (((1,), (1,)), ((), ())), preferred_element_type=jnp.float32)


def t_dot(a, b):
    return lax.dot_general(a, b, (((0,), (0,)), ((), ())), preferred_element_type=jnp.float32)


def forward(own, others, backs_cuts, w_gate, w_up, w_down, chunk):
    experts, rows, width = own.shape
    hidden = w_gate.shape[1]
    steps = width // chunk
    count = len(others)

    def kernel(own_ref, *refs):
        other_refs, (wg_ref, wu_ref, wd_ref) = refs[:count], refs[count : count + 3]
        own_out, *other_outs, hidden_ref, gate_sum, up_sum, active_ref = refs[count + 3 :]
        step = pl.program_id(1)

        @pl.when(step < steps)
        def _():
            block = jnp.concatenate([own_ref[0]] + [ref[0] for ref in other_refs], 0)
            gate = dot_t(block, wg_ref[0])
            up = dot_t(block, wu_ref[0])

            @pl.when(step == 0)
            def _():
                gate_sum[...] = gate
                up_sum[...] = up

            @pl.when(step > 0)
            def _():
                gate_sum[...] += gate
                up_sum[...] += up

        @pl.when(step == steps)
        def _():
            gate, up = gate_sum[...], up_sum[...]
            hidden_ref[0, 0] = gate
            hidden_ref[0, 1] = up
            active_ref[...] = (gate * jax.nn.sigmoid(gate) * up).astype(jnp.bfloat16)

        @pl.when(step >= steps)
        def _():
            out = jnp.dot(active_ref[...], wd_ref[0], preferred_element_type=jnp.float32)
            out = out.astype(jnp.bfloat16)
            own_out[0] = out[:rows]
            at = rows
            for other_out in other_outs:
                other_out[0] = out[at : at + other_out.shape[1]]
                at += other_out.shape[1]

    def early(e, s):
        return (e, 0, jnp.minimum(s, steps - 1))

    def late(e, s):
        return (e, 0, jnp.maximum(s - steps, 0))

    row_block = pl.BlockSpec((1, rows, chunk), early)
    weight_block = pl.BlockSpec((1, hidden, chunk), early)
    out, *backs, values = call(
        kernel,
        (experts, 2 * steps),
        (own, *others, w_gate, w_up, w_down),
        [row_block]
        + [pl.BlockSpec((1, other.shape[1], chunk), early) for other in others]
        + [weight_block, weight_block, pl.BlockSpec((1, hidden, chunk), late)],
        [shape(own.shape)] + [shape((experts, cut, width)) for cut in backs_cuts]
        + [shape((experts, 2, 2 * rows, hidden), jnp.float32)],
        [
            pl.BlockSpec((1, rows, chunk), late),
            *[pl.BlockSpec((1, cut, chunk), late) for cut in backs_cuts],
            pl.BlockSpec((1, 2, 2 * rows, hidden), lambda e, s: (e, 0, 0, 0)),
        ],
        12 * experts * rows * hidden * width,
        [
            pltpu.VMEM((2 * rows, hidden), jnp.float32),
            pltpu.VMEM((2 * rows, hidden), jnp.float32),
            pltpu.VMEM((2 * rows, hidden), jnp.bfloat16),
        ],
    )
    return out, backs, values


def back_act(grads, w_down, chunk):
    experts, _, width = grads[0].shape
    rows = sum(part.shape[1] for part in grads)
    hidden = w_down.shape[1]

    def kernel(*refs):
        wd_ref, out_ref = refs[-2:]
        found = dot_t(jnp.concatenate([ref[0] for ref in refs[:-2]], 0), wd_ref[0])

        @pl.when(pl.program_id(1) == 0)
        def _():
            out_ref[0] = found

        @pl.when(pl.program_id(1) > 0)
        def _():
            out_ref[0] += found

    return call(
        kernel,
        (experts, width // chunk),
        (*grads, w_down),
        [pl.BlockSpec((1, part.shape[1], chunk), lambda e, s: (e, 0, s)) for part in grads]
        + [pl.BlockSpec((1, hidden, chunk), lambda e, s: (e, 0, s))],
        [shape((experts, rows, hidden), jnp.float32)],
        [pl.BlockSpec((1, rows, hidden), lambda e, s: (e, 0, 0))],
        2 * experts * rows * hidden * width,
        told=True,
    )[0]


def hidden_of(refs, which):
    halves = [[], []]
    for ref in refs:
        rows = ref.shape[2] // 2
        for side in range(2):
            halves[side].append(ref[0, which, side * rows : (side + 1) * rows, :])
    return jnp.concatenate(halves[0] + halves[1], 0)


def down_grad(grads, hiddens, chunk):
    experts, _, width = grads[0].shape
    rows = sum(part.shape[1] for part in grads)
    units = hiddens[0].shape[3]
    count = len(grads)

    def kernel(*refs):
        hidden_refs, out_ref, active_ref = refs[count:-2], refs[-2], refs[-1]

        @pl.when(pl.program_id(1) == 0)
        def _():
            gate, up = hidden_of(hidden_refs, 0), hidden_of(hidden_refs, 1)
            active_ref[...] = (gate * jax.nn.sigmoid(gate) * up).astype(jnp.bfloat16)

        block = jnp.concatenate([ref[0] for ref in refs[:count]], 0)
        out_ref[0] = t_dot(active_ref[...], block).astype(jnp.bfloat16)

    return call(
        kernel,
        (experts, width // chunk),
        (*grads, *hiddens),
        [pl.BlockSpec((1, part.shape[1], chunk), lambda e, s: (e, 0, s)) for part in grads]
        + [pl.BlockSpec((1,) + h.shape[1:], lambda e, s: (e, 0, 0, 0)) for h in hiddens],
        [shape((experts, units, width))],
        [pl.BlockSpec((1, units, chunk), lambda e, s: (e, 0, s))],
        2 * experts * rows * units * width,
        [pltpu.VMEM((rows, units), jnp.bfloat16)],
        told=True,
    )[0]


def up_grads(back, ordered, hiddens, chunk):
    experts, rows, units = back.shape
    width = ordered[0].shape[2]
    count = len(ordered)

    def kernel(back_ref, *refs):
        row_refs, hidden_refs = refs[:count], refs[count:-4]
        dg_ref, du_ref, dgate, dup = refs[-4:]

        @pl.when(pl.program_id(1) == 0)
        def _():
            gate, up = hidden_of(hidden_refs, 0), hidden_of(hidden_refs, 1)
            sig = jax.nn.sigmoid(gate)
            d_act = back_ref[0]
            dgate[...] = (d_act * up * sig * (1.0 + gate * (1.0 - sig))).astype(jnp.bfloat16)
            dup[...] = (d_act * (gate * sig)).astype(jnp.bfloat16)

        block = jnp.concatenate([ref[0] for ref in row_refs], 0)
        dg_ref[0] = t_dot(dgate[...], block).astype(jnp.bfloat16)
        du_ref[0] = t_dot(dup[...], block).astype(jnp.bfloat16)

    out_block = pl.BlockSpec((1, units, chunk), lambda e, s: (e, 0, s))
    return call(
        kernel,
        (experts, width // chunk),
        (back, *ordered, *hiddens),
        [pl.BlockSpec((1, rows, units), lambda e, s: (e, 0, 0))]
        + [pl.BlockSpec((1, o.shape[1], chunk), lambda e, s: (e, 0, s)) for o in ordered]
        + [pl.BlockSpec((1,) + h.shape[1:], lambda e, s: (e, 0, 0, 0)) for h in hiddens],
        [shape((experts, units, width))] * 2,
        [out_block] * 2,
        4 * experts * rows * units * width,
        [pltpu.VMEM((rows, units), jnp.bfloat16)] * 2,
        told=True,
    )


def attend(base, queries, pairs, out_proj):
    rows, width = queries.shape[0], out_proj.shape[1]
    tokens = pairs.shape[0]
    steps = queries.shape[1] // (2 * HEAD)

    def kernel(base_ref, query_ref, pairs_ref, proj_ref, out_ref, sum_ref):
        both = query_ref[...]
        query = jnp.concatenate([both[:, :HEAD], both[:, HEAD:]], 0)
        pairs = pairs_ref[...]
        scores = dot_t(query, pairs[:, :HEAD]) * (1.0 / math.sqrt(HEAD))
        query_pos = lax.broadcasted_iota(jnp.int32, (2 * rows, 1), 0) % rows + base_ref[0]
        key_pos = lax.broadcasted_iota(jnp.int32, (1, tokens), 1)
        scores = jnp.where(key_pos <= query_pos, scores, -1e30)
        probs = jnp.exp(scores - jnp.max(scores, axis=1, keepdims=True))
        denom = jnp.sum(probs, axis=1, keepdims=True)
        heads = jnp.dot(
            probs.astype(jnp.bfloat16), pairs[:, HEAD:], preferred_element_type=jnp.float32
        )
        heads = (heads / denom).astype(jnp.bfloat16)
        attn = jnp.concatenate([heads[:rows], heads[rows:]], 1)
        part = jnp.dot(attn, proj_ref[...], preferred_element_type=jnp.float32)
        step = pl.program_id(0)

        @pl.when(step == 0)
        def _():
            sum_ref[...] = part

        @pl.when(step > 0)
        def _():
            sum_ref[...] += part

        @pl.when(step == steps - 1)
        def _():
            out_ref[...] = sum_ref[...].astype(jnp.bfloat16)

    return call(
        kernel,
        (steps,),
        (base, queries, pairs, out_proj),
        [
            pl.BlockSpec(memory_space=pltpu.SMEM),
            pl.BlockSpec((rows, 2 * HEAD), lambda h: (0, h)),
            pl.BlockSpec((tokens, 2 * HEAD), lambda h: (0, 0)),
            pl.BlockSpec((2 * HEAD, width), lambda h: (h, 0)),
        ],
        [shape((rows, width))],
        [pl.BlockSpec((rows, width), lambda h: (0, 0))],
        2 * rows * queries.shape[1] * (2 * tokens + width),
        [pltpu.VMEM((rows, width), jnp.float32)],
        limit=56,
    )[0]


def shards(
    queries,
    keys,
    values,
    resid,
    out_proj,
    norm_gain,
    expert_ids,
    gates,
    w_gate,
    w_up,
    w_down,
    cotangent,
):
    width = resid.shape[1]
    chunk = min(512, width)
    yh, z, k, yl = (lax.axis_index(name) for name in ("yh", "z", "k", "yl"))
    ctx = ((yh * 4 + z) * 2 + k).astype(jnp.int32)

    tok_ctx = queries.shape[0]
    key_mine = lax.dynamic_slice_in_dim(keys, yl * HEAD, HEAD, 1)
    value_mine = lax.dynamic_slice_in_dim(values, yl * HEAD, HEAD, 1)
    pair = jnp.concatenate([key_mine, value_mine], 1)
    pairs = lax.all_to_all(
        jnp.broadcast_to(pair, (16,) + pair.shape), ("yh", "z", "k"), 0, 0, tiled=True
    ).reshape(16 * tok_ctx, 2 * HEAD)

    rest = gates
    pieces = [expert_ids.astype(jnp.bfloat16)]
    for _ in range(3):
        piece = lax.reduce_precision(rest, 8, 7)
        pieces.append(piece.astype(jnp.bfloat16))
        rest = rest - piece
    pieces.append(jnp.zeros((ROWS, META - 4 * TOPK), jnp.bfloat16))
    meta = jnp.concatenate(pieces, 1)
    cot_near = jnp.concatenate(gather_step(cotangent, stage_dims(0)), 0)
    cot_near = jnp.concatenate(gather_step(after(cot_near, pairs), stage_dims(1)), 0)
    cot_sides = gather_sides(cot_near)

    base = (ctx * tok_ctx).reshape(1)
    mixed = attend(base, queries, pairs, out_proj)
    mixed = lax.all_to_all(mixed, ("yl", "x"), 0, 0, tiled=True).reshape(8, ROWS, width)
    stream = resid.astype(jnp.float32) + jnp.sum(mixed.astype(jnp.float32), axis=0)
    normed = (
        stream * lax.rsqrt(jnp.mean(stream * stream, axis=1, keepdims=True) + 1e-06) * norm_gain
    ).astype(jnp.bfloat16)

    me = ctx.reshape(1)
    near = jnp.concatenate(
        gather_step(jnp.concatenate([normed, meta], 1), stage_dims(0)), 0
    )
    near = after(jnp.concatenate(gather_step(near, stage_dims(1)), 0), *cot_sides)
    left, right = gather_sides(near)
    half = near.shape[0] // 2
    narrow, wide = 2 * chunk, 4 * chunk

    slots = near.shape[0] // ROWS * CAP
    cuts = [slots // 32 * 16 + 16, slots // 32 * 16]
    thirds = [cuts[0], 2 * cuts[1], cuts[0]]

    def run_forward(rows_own, rows_got, backs):
        return forward(rows_own, rows_got, backs, w_gate, w_up, w_down, wide)

    own0, other0, place0, weight0 = pack_rows(me, [[near]], [slots], width, narrow)
    got0 = swap_cores(other0)
    out0, back0, hidden0 = run_forward(own0, got0, [slots])
    back0 = swap_cores(back0)
    left, right = after(left, out0), after(right, out0)

    far_a, far_b = gather_far(left, right)
    own1, other1, place1, weight1 = pack_rows(me, [[left], [right]], thirds, width, narrow)
    got1 = swap_cores(other1)
    (sum0,) = merge(place0, weight0, after(out0, *other1), back0, [(2 * half, 2 * half, 0)], narrow)
    out1, back1, hidden1 = run_forward(after(own1, sum0), got1, [2 * slots])
    back1 = swap_cores(back1)

    cot_left, cot_right = (after(side, far_a) for side in cot_sides)
    cot_far = gather_far(cot_left, cot_right)
    far_a, far_b = after(far_a, out1), after(far_b, out1)
    own2, other2, place2, weight2 = pack_rows(me, [[far_a, far_b]], cuts, width, narrow)
    got2 = swap_cores(other2)
    out2, back2, hidden2 = run_forward(own2, got2, cuts)
    back2 = swap_cores(back2)

    dims = stage_dims(2)
    left_a, left_b, right_a, right_b = merge(
        place1, weight1, after(out1, out2), back1, [(half, half, 0)] * 4, narrow
    )
    out2 = after(out2, left_a, *cot_far)
    far_a, far_b = merge(place2, weight2, out2, back2, [(half, half, 0)] * 2, narrow)
    got_far_a, got_far_b = send(far_a, dims, -1), send(far_b, dims, 1)
    got_left_b, got_right_a = send(left_b, dims, -1), send(right_a, dims, 1)

    cot_tiles = [[cot_near], [cot_left], [cot_right], list(cot_far)]
    places, weights = (place0, place1, place2), (weight0, weight1, weight2)
    grads_own, grads_other = pack_grads(places, weights, cot_tiles, chunk)
    grads = [grads_own] + swap_cores(after_all(grads_other, got_left_b, got_right_a))
    hiddens = [hidden0, hidden1, hidden2]

    left_a = add(left_a, got_far_a).astype(jnp.bfloat16)
    right_b = add(right_b, got_far_b).astype(jnp.bfloat16)
    got_left_a, got_right_b = send(left_a, dims, -1), send(right_b, dims, 1)
    back = back_act(grads, w_down, wide)
    total = jnp.concatenate(
        [
            add(sum0[:half], got_left_a, got_right_a),
            add(sum0[half:], got_left_b, got_right_b),
        ],
        0,
    )
    grad_down = down_grad(after_all(grads, back), hiddens, narrow)
    rows = [own0, own1, own2] + got0 + got1 + got2
    grad_gate, grad_up = up_grads(back, rows, hiddens, narrow)
    combined = scatter_near(total)
    layer_out = (stream + combined).astype(jnp.bfloat16)
    return layer_out, grad_gate, grad_up, grad_down


def solution(mesh):
    split = Mesh(mesh.devices.reshape(SIZES), AXES)
    ctx, tp = ("yh", "z", "k"), ("yl", "x")
    rows, weights = P(ctx + tp, None), P(ctx, tp, None)
    in_specs = (
        P(ctx, tp),
        P(ctx, None),
        P(ctx, None),
        rows,
        P(tp, None),
        P(),
        rows,
        rows,
        weights,
        weights,
        weights,
        rows,
    )
    return jax.shard_map(
        shards,
        mesh=split,
        in_specs=in_specs,
        out_specs=(rows, weights, weights, weights),
        check_vma=False,
    )
```

```python
import math

import jax
import jax.numpy as jnp
from jax import lax
from jax.experimental import pallas as pl
from jax.experimental.pallas import tpu as pltpu
from jax.sharding import Mesh
from jax.sharding import PartitionSpec as P

QHEADS = 32
KVHEADS = 2
HEAD = 128
TOPK = 8
CAP = 5
ROWS = 16
META = 128
SIZES = (2, 4, 2, 2, 4)
AXES = ("yh", "z", "k", "yl", "x")


def device_index(yh, z, k, yl, x):
    return (((yh * 4 + z) * 2 + k) * 2 + yl) * 4 + x


def shifted(dims, step):
    pairs = []
    for x in range(4):
        for y in range(4):
            for z in range(4):
                for k in range(2):
                    at = {"x": x, "y": y, "z": z}
                    to = dict(at)
                    to[dims[k]] = (to[dims[k]] + step) % 4
                    pairs.append(
                        (
                            device_index(at["y"] // 2, at["z"], k, at["y"] % 2, at["x"]),
                            device_index(to["y"] // 2, to["z"], k, to["y"] % 2, to["x"]),
                        )
                    )
    return pairs


def send(array, dims, step):
    return lax.ppermute(array, AXES, shifted(dims, step))


def swap_cores(arrays):
    return [lax.ppermute(array, "k", [(0, 1), (1, 0)]) for array in arrays]


def gather_step(block, dims):
    return [block, send(block, dims, 1), send(block, dims, -1), send(block, dims, 2)]


ORDERS = ("xyz", "zxy")


def stage_dims(stage):
    return (ORDERS[0][stage], ORDERS[1][stage])


def after(array, *others):
    return lax.optimization_barrier((array,) + others)[0]


def after_all(arrays, *others):
    return tuple(after(array, *others) for array in arrays)


def gather_near(block):
    for stage in range(2):
        block = jnp.concatenate(gather_step(block, stage_dims(stage)), 0)
    return block


def gather_sides(block):
    dims = stage_dims(2)
    return send(block, dims, 1), send(block, dims, -1)


def gather_far(left, right):
    dims = stage_dims(2)
    half = left.shape[0] // 2
    return send(left[:half], dims, 1), send(right[half:], dims, -1)


def add(*terms):
    total = terms[0].astype(jnp.float32)
    for term in terms[1:]:
        total = total + term.astype(jnp.float32)
    return total


def scatter_near(total):
    for stage in (1, 0):
        dims = stage_dims(stage)
        parts = total.astype(jnp.bfloat16).reshape(4, -1, total.shape[1])
        total = add(
            parts[0], send(parts[1], dims, -1), send(parts[2], dims, 1), send(parts[3], dims, -2)
        )
    return total


def placement(meta, experts, me):
    rows = meta.shape[0]
    slots = rows // ROWS * CAP
    turned = meta.astype(jnp.float32).T
    ids = turned[0:TOPK]
    gates = turned[TOPK : 2 * TOPK] + turned[2 * TOPK : 3 * TOPK] + turned[3 * TOPK : 4 * TOPK]
    token = lax.broadcasted_iota(jnp.int32, (rows, rows), 0)
    later = lax.broadcasted_iota(jnp.int32, (rows, rows), 1)
    earlier = ((token // ROWS == later // ROWS) & (token < later)).astype(jnp.float32)
    block = (lax.broadcasted_iota(jnp.int32, (1, rows), 1) // ROWS).astype(jnp.float32)
    slot_at = lax.broadcasted_iota(jnp.int32, (slots, rows), 0).astype(jnp.float32)
    places, weights = [], []
    for side in range(2):
        for local in range(experts):
            expert = ((me ^ side) * experts + local).astype(jnp.float32)
            named = ids == expert
            hit = jnp.max(named.astype(jnp.float32), axis=0, keepdims=True)
            gate = jnp.sum(jnp.where(named, gates, 0.0), axis=0, keepdims=True)
            rank = jnp.dot(
                jnp.broadcast_to(hit, (8, rows)), earlier, preferred_element_type=jnp.float32
            )[0:1]
            slot = jnp.where(hit > 0.0, block * CAP + rank, -1.0)
            place = (slot_at == slot).astype(jnp.float32)
            places.append(place)
            weights.append(jnp.sum(place * gate, axis=1, keepdims=True))
    return jnp.concatenate(places, 0), jnp.concatenate(weights, 0)


def cost(flops, *arrays):
    moved = sum(array.size * array.dtype.itemsize for array in arrays)
    return pl.CostEstimate(flops=int(flops), bytes_accessed=int(moved), transcendentals=0)


def call(kernel, grid, ins, in_specs, outs, out_specs, flops, scratch=(), limit=24, told=False):
    return pl.pallas_call(
        kernel,
        grid=grid,
        in_specs=in_specs,
        out_specs=out_specs,
        out_shape=outs,
        scratch_shapes=list(scratch),
        compiler_params=pltpu.CompilerParams(vmem_limit_bytes=limit * 1024 * 1024),
        cost_estimate=cost(flops, *ins, *outs) if told else None,
    )(*ins)


def shape(dims, dtype=jnp.bfloat16):
    return jax.ShapeDtypeStruct(dims, dtype)


def joined(refs):
    return refs[0][...] if len(refs) == 1 else jnp.concatenate([ref[...] for ref in refs], 0)


def store_slots(found, own_ref, other_refs):
    slots = found[0].shape[0] // 4
    for e in range(2):
        own_ref[e] = jnp.concatenate([tile[e * slots : (e + 1) * slots] for tile in found], 0)
        rows = jnp.concatenate([tile[(e + 2) * slots : (e + 3) * slots] for tile in found], 0)
        at = 0
        for ref in other_refs:
            ref[e] = rows[at : at + ref.shape[1]]
            at += ref.shape[1]


def pack_rows(me, groups, cuts, width, chunk):
    parts = [part for group in groups for part in group]
    tile_rows = sum(part.shape[0] for part in groups[0])
    slots = tile_rows // ROWS * CAP
    count, total = len(groups), len(parts)
    meta_at = width // META

    def kernel(me_ref, *refs):
        metas, rows = refs[:total], refs[total : 2 * total]
        own_ref, *other_refs, place_ref, weight_ref = refs[2 * total :]

        @pl.when(pl.program_id(0) == 0)
        def _():
            at = 0
            for tile, group in enumerate(groups):
                meta = joined(metas[at : at + len(group)])
                at += len(group)
                place, weight = placement(meta, 2, me_ref[0])
                place_ref[tile] = place.astype(jnp.bfloat16)
                weight_ref[tile] = jnp.broadcast_to(weight, weight_ref.shape[1:])

        at, found = 0, []
        for tile, group in enumerate(groups):
            block = joined(rows[at : at + len(group)])
            at += len(group)
            rows_of = jnp.dot(place_ref[tile], block, preferred_element_type=jnp.float32)
            found.append(rows_of.astype(jnp.bfloat16))
        store_slots(found, own_ref, other_refs)

    own, *others, place, weight = call(
        kernel,
        (width // chunk,),
        (me, *parts, *parts),
        [pl.BlockSpec(memory_space=pltpu.SMEM)]
        + [pl.BlockSpec((part.shape[0], META), lambda j: (0, meta_at)) for part in parts]
        + [pl.BlockSpec((part.shape[0], chunk), lambda j: (0, j)) for part in parts],
        [shape((2, count * slots, width))]
        + [shape((2, cut, width)) for cut in cuts]
        + [
            shape((count, 4 * slots, tile_rows)),
            shape((count, 4 * slots, META), jnp.float32),
        ],
        [pl.BlockSpec((2, count * slots, chunk), lambda j: (0, 0, j))]
        + [pl.BlockSpec((2, cut, chunk), lambda j: (0, 0, j)) for cut in cuts]
        + [
            pl.BlockSpec((count, 4 * slots, tile_rows), lambda j: (0, 0, 0)),
            pl.BlockSpec((count, 4 * slots, META), lambda j: (0, 0, 0)),
        ],
        2 * count * 4 * slots * tile_rows * width,
    )
    return own, others, place, weight


def pack_grads(places, weights, tiles, chunk):
    parts = [part for group in tiles for part in group]
    width = parts[0].shape[1]
    tile_rows = places[0].shape[2]
    slots = places[0].shape[1] // 4
    count = len(places)

    def kernel(*refs):
        place_refs, weight_refs = refs[:count], refs[count : 2 * count]
        rows = refs[2 * count : 2 * count + len(parts)]
        own_ref, *other_refs = refs[2 * count + len(parts) :]
        placed = [ref[t] for ref in place_refs for t in range(ref.shape[0])]
        scales = [ref[t] for ref in weight_refs for t in range(ref.shape[0])]
        at, found = 0, []
        for tile, group in enumerate(tiles):
            block = joined(rows[at : at + len(group)])
            at += len(group)
            rows_of = jnp.dot(placed[tile], block, preferred_element_type=jnp.float32)
            found.append((rows_of * scales[tile][:, 0:1]).astype(jnp.bfloat16))
        store_slots(found, own_ref, other_refs)

    own, *others = call(
        kernel,
        (width // chunk,),
        (*places, *weights, *parts),
        [pl.BlockSpec(a.shape, lambda j: (0, 0, 0)) for a in (*places, *weights)]
        + [pl.BlockSpec((part.shape[0], chunk), lambda j: (0, j)) for part in parts],
        [shape((2, len(tiles) * slots, width))] + [shape((2, slots, width))] * len(tiles),
        [pl.BlockSpec((2, len(tiles) * slots, chunk), lambda j: (0, 0, j))]
        + [pl.BlockSpec((2, slots, chunk), lambda j: (0, 0, j))] * len(tiles),
        2 * len(tiles) * 4 * slots * tile_rows * width,
        told=True,
    )
    return own, others


def merge(place, weight, own, others, pieces, chunk, into=()):
    width = own.shape[2]
    rows = place.shape[2]
    slots = place.shape[1] // 4
    count = own.shape[1] // slots

    def kernel(place_ref, weight_ref, own_ref, *refs):
        outs = refs[len(others) + len(into) :]
        other_rows = [
            jnp.concatenate([ref[e] for ref in refs[: len(others)]], 0) for e in range(2)
        ]
        totals = []
        for tile in range(count):
            span = pl.ds(tile * slots, slots)
            block = jnp.concatenate(
                [own_ref[e, span, :] for e in range(2)]
                + [rows_of[tile * slots : (tile + 1) * slots] for rows_of in other_rows],
                0,
            )
            scale = weight_ref[tile][:, 0:1]
            scaled = (block.astype(jnp.float32) * scale).astype(jnp.bfloat16)
            totals.append(t_dot(place_ref[tile], scaled).astype(jnp.bfloat16))
        at = 0
        for out, (size, _, _) in zip(outs, pieces):
            out[...] = totals[at // rows][at % rows : at % rows + size]
            at += size

    return pl.pallas_call(
        kernel,
        grid=(width // chunk,),
        in_specs=[
            pl.BlockSpec(place.shape, lambda j: (0, 0, 0)),
            pl.BlockSpec(weight.shape, lambda j: (0, 0, 0)),
            pl.BlockSpec((2, own.shape[1], chunk), lambda j: (0, 0, j)),
        ]
        + [pl.BlockSpec((2, other.shape[1], chunk), lambda j: (0, 0, j)) for other in others]
        + [pl.BlockSpec(memory_space=pl.ANY)] * len(into),
        out_specs=[
            pl.BlockSpec((size, chunk), lambda j, at=at: (at, j)) for size, _, at in pieces
        ],
        out_shape=[shape((total, width)) for _, total, _ in pieces],
        input_output_aliases={3 + len(others) + i: i for i in range(len(into))},
        compiler_params=pltpu.CompilerParams(vmem_limit_bytes=24 * 1024 * 1024),
    )(place, weight, own, *others, *into)


def dot_t(a, b):
    return lax.dot_general(a, b, (((1,), (1,)), ((), ())), preferred_element_type=jnp.float32)


def t_dot(a, b):
    return lax.dot_general(a, b, (((0,), (0,)), ((), ())), preferred_element_type=jnp.float32)


def forward(own, others, backs_cuts, w_gate, w_up, w_down, chunk):
    experts, rows, width = own.shape
    hidden = w_gate.shape[1]
    steps = width // chunk
    count = len(others)

    def kernel(own_ref, *refs):
        other_refs, (wg_ref, wu_ref, wd_ref) = refs[:count], refs[count : count + 3]
        own_out, *other_outs, hidden_ref, gate_sum, up_sum, active_ref = refs[count + 3 :]
        step = pl.program_id(1)

        @pl.when(step < steps)
        def _():
            block = jnp.concatenate([own_ref[0]] + [ref[0] for ref in other_refs], 0)
            gate = dot_t(block, wg_ref[0])
            up = dot_t(block, wu_ref[0])

            @pl.when(step == 0)
            def _():
                gate_sum[...] = gate
                up_sum[...] = up

            @pl.when(step > 0)
            def _():
                gate_sum[...] += gate
                up_sum[...] += up

        @pl.when(step == steps)
        def _():
            gate, up = gate_sum[...], up_sum[...]
            hidden_ref[0, 0] = gate
            hidden_ref[0, 1] = up
            active_ref[...] = (gate * jax.nn.sigmoid(gate) * up).astype(jnp.bfloat16)

        @pl.when(step >= steps)
        def _():
            out = jnp.dot(active_ref[...], wd_ref[0], preferred_element_type=jnp.float32)
            out = out.astype(jnp.bfloat16)
            own_out[0] = out[:rows]
            at = rows
            for other_out in other_outs:
                other_out[0] = out[at : at + other_out.shape[1]]
                at += other_out.shape[1]

    def early(e, s):
        return (e, 0, jnp.minimum(s, steps - 1))

    def late(e, s):
        return (e, 0, jnp.maximum(s - steps, 0))

    row_block = pl.BlockSpec((1, rows, chunk), early)
    weight_block = pl.BlockSpec((1, hidden, chunk), early)
    out, *backs, values = call(
        kernel,
        (experts, 2 * steps),
        (own, *others, w_gate, w_up, w_down),
        [row_block]
        + [pl.BlockSpec((1, other.shape[1], chunk), early) for other in others]
        + [weight_block, weight_block, pl.BlockSpec((1, hidden, chunk), late)],
        [shape(own.shape)] + [shape((experts, cut, width)) for cut in backs_cuts]
        + [shape((experts, 2, 2 * rows, hidden), jnp.float32)],
        [
            pl.BlockSpec((1, rows, chunk), late),
            *[pl.BlockSpec((1, cut, chunk), late) for cut in backs_cuts],
            pl.BlockSpec((1, 2, 2 * rows, hidden), lambda e, s: (e, 0, 0, 0)),
        ],
        12 * experts * rows * hidden * width,
        [
            pltpu.VMEM((2 * rows, hidden), jnp.float32),
            pltpu.VMEM((2 * rows, hidden), jnp.float32),
            pltpu.VMEM((2 * rows, hidden), jnp.bfloat16),
        ],
    )
    return out, backs, values


def back_act(grads, w_down, chunk):
    experts, _, width = grads[0].shape
    rows = sum(part.shape[1] for part in grads)
    hidden = w_down.shape[1]

    def kernel(*refs):
        wd_ref, out_ref = refs[-2:]
        found = dot_t(jnp.concatenate([ref[0] for ref in refs[:-2]], 0), wd_ref[0])

        @pl.when(pl.program_id(1) == 0)
        def _():
            out_ref[0] = found

        @pl.when(pl.program_id(1) > 0)
        def _():
            out_ref[0] += found

    return call(
        kernel,
        (experts, width // chunk),
        (*grads, w_down),
        [pl.BlockSpec((1, part.shape[1], chunk), lambda e, s: (e, 0, s)) for part in grads]
        + [pl.BlockSpec((1, hidden, chunk), lambda e, s: (e, 0, s))],
        [shape((experts, rows, hidden), jnp.float32)],
        [pl.BlockSpec((1, rows, hidden), lambda e, s: (e, 0, 0))],
        2 * experts * rows * hidden * width,
        told=True,
    )[0]


def hidden_of(refs, which):
    halves = [[], []]
    for ref in refs:
        rows = ref.shape[2] // 2
        for side in range(2):
            halves[side].append(ref[0, which, side * rows : (side + 1) * rows, :])
    return jnp.concatenate(halves[0] + halves[1], 0)


def down_grad(grads, hiddens, chunk):
    experts, _, width = grads[0].shape
    rows = sum(part.shape[1] for part in grads)
    units = hiddens[0].shape[3]
    count = len(grads)

    def kernel(*refs):
        hidden_refs, out_ref, active_ref = refs[count:-2], refs[-2], refs[-1]

        @pl.when(pl.program_id(1) == 0)
        def _():
            gate, up = hidden_of(hidden_refs, 0), hidden_of(hidden_refs, 1)
            active_ref[...] = (gate * jax.nn.sigmoid(gate) * up).astype(jnp.bfloat16)

        block = jnp.concatenate([ref[0] for ref in refs[:count]], 0)
        out_ref[0] = t_dot(active_ref[...], block).astype(jnp.bfloat16)

    return call(
        kernel,
        (experts, width // chunk),
        (*grads, *hiddens),
        [pl.BlockSpec((1, part.shape[1], chunk), lambda e, s: (e, 0, s)) for part in grads]
        + [pl.BlockSpec((1,) + h.shape[1:], lambda e, s: (e, 0, 0, 0)) for h in hiddens],
        [shape((experts, units, width))],
        [pl.BlockSpec((1, units, chunk), lambda e, s: (e, 0, s))],
        2 * experts * rows * units * width,
        [pltpu.VMEM((rows, units), jnp.bfloat16)],
        told=True,
    )[0]


def up_grads(back, ordered, hiddens, chunk):
    experts, rows, units = back.shape
    width = ordered[0].shape[2]
    count = len(ordered)

    def kernel(back_ref, *refs):
        row_refs, hidden_refs = refs[:count], refs[count:-4]
        dg_ref, du_ref, dgate, dup = refs[-4:]

        @pl.when(pl.program_id(1) == 0)
        def _():
            gate, up = hidden_of(hidden_refs, 0), hidden_of(hidden_refs, 1)
            sig = jax.nn.sigmoid(gate)
            d_act = back_ref[0]
            dgate[...] = (d_act * up * sig * (1.0 + gate * (1.0 - sig))).astype(jnp.bfloat16)
            dup[...] = (d_act * (gate * sig)).astype(jnp.bfloat16)

        block = jnp.concatenate([ref[0] for ref in row_refs], 0)
        dg_ref[0] = t_dot(dgate[...], block).astype(jnp.bfloat16)
        du_ref[0] = t_dot(dup[...], block).astype(jnp.bfloat16)

    out_block = pl.BlockSpec((1, units, chunk), lambda e, s: (e, 0, s))
    return call(
        kernel,
        (experts, width // chunk),
        (back, *ordered, *hiddens),
        [pl.BlockSpec((1, rows, units), lambda e, s: (e, 0, 0))]
        + [pl.BlockSpec((1, o.shape[1], chunk), lambda e, s: (e, 0, s)) for o in ordered]
        + [pl.BlockSpec((1,) + h.shape[1:], lambda e, s: (e, 0, 0, 0)) for h in hiddens],
        [shape((experts, units, width))] * 2,
        [out_block] * 2,
        4 * experts * rows * units * width,
        [pltpu.VMEM((rows, units), jnp.bfloat16)] * 2,
        told=True,
    )


def attend(base, queries, blocks, positions, out_proj):
    rows, width = queries.shape[0], out_proj.shape[1]
    tokens = positions.shape[1]
    steps = queries.shape[1] // (2 * HEAD)

    def kernel(base_ref, query_ref, first_ref, second_ref, pos_ref, proj_ref, out_ref, sum_ref):
        both = query_ref[...]
        query = jnp.concatenate([both[:, :HEAD], both[:, HEAD:]], 0)
        pairs = jnp.concatenate([first_ref[...], second_ref[...]], 0)
        scores = dot_t(query, pairs[:, :HEAD]) * (1.0 / math.sqrt(HEAD))
        query_pos = lax.broadcasted_iota(jnp.int32, (2 * rows, 1), 0) % rows + base_ref[0]
        scores = jnp.where(pos_ref[...] <= query_pos, scores, -1e30)
        probs = jnp.exp(scores - jnp.max(scores, axis=1, keepdims=True))
        denom = jnp.sum(probs, axis=1, keepdims=True)
        heads = jnp.dot(
            probs.astype(jnp.bfloat16), pairs[:, HEAD:], preferred_element_type=jnp.float32
        )
        heads = (heads / denom).astype(jnp.bfloat16)
        attn = jnp.concatenate([heads[:rows], heads[rows:]], 1)
        part = jnp.dot(attn, proj_ref[...], preferred_element_type=jnp.float32)
        step = pl.program_id(0)

        @pl.when(step == 0)
        def _():
            sum_ref[...] = part

        @pl.when(step > 0)
        def _():
            sum_ref[...] += part

        @pl.when(step == steps - 1)
        def _():
            out_ref[...] = sum_ref[...].astype(jnp.bfloat16)

    half = pl.BlockSpec((tokens // 2, 2 * HEAD), lambda h: (0, 0))
    return call(
        kernel,
        (steps,),
        (base, queries, *blocks, positions, out_proj),
        [
            pl.BlockSpec(memory_space=pltpu.SMEM),
            pl.BlockSpec((rows, 2 * HEAD), lambda h: (0, h)),
            half,
            half,
            pl.BlockSpec((1, tokens), lambda h: (0, 0)),
            pl.BlockSpec((2 * HEAD, width), lambda h: (h, 0)),
        ],
        [shape((rows, width))],
        [pl.BlockSpec((rows, width), lambda h: (0, 0))],
        2 * rows * queries.shape[1] * (2 * tokens + width),
        [pltpu.VMEM((rows, width), jnp.float32)],
        limit=56,
    )[0]


def key_positions(tok_ctx):
    k = lax.axis_index("k")
    groups = jnp.concatenate([2 * jnp.arange(8) + k, 2 * jnp.arange(8) + (1 - k)]).astype(jnp.int32)
    return (groups[:, None] * tok_ctx + jnp.arange(tok_ctx, dtype=jnp.int32)[None, :]).reshape(1, -1)


def shards(
    queries,
    keys,
    values,
    resid,
    out_proj,
    norm_gain,
    expert_ids,
    gates,
    w_gate,
    w_up,
    w_down,
    cotangent,
):
    width = resid.shape[1]
    chunk = min(512, width)
    yh, z, k, yl = (lax.axis_index(name) for name in ("yh", "z", "k", "yl"))
    ctx = ((yh * 4 + z) * 2 + k).astype(jnp.int32)

    tok_ctx = queries.shape[0]
    key_mine = lax.dynamic_slice_in_dim(keys, yl * HEAD, HEAD, 1)
    value_mine = lax.dynamic_slice_in_dim(values, yl * HEAD, HEAD, 1)
    pair = jnp.concatenate([key_mine, value_mine], 1)
    pairs = lax.all_to_all(
        jnp.broadcast_to(pair, (8,) + pair.shape), ("yh", "z"), 0, 0, tiled=True
    ).reshape(8 * tok_ctx, 2 * HEAD)
    blocks = [pairs] + swap_cores([pairs])

    rest = gates
    pieces = [expert_ids.astype(jnp.bfloat16)]
    for _ in range(3):
        piece = lax.reduce_precision(rest, 8, 7)
        pieces.append(piece.astype(jnp.bfloat16))
        rest = rest - piece
    pieces.append(jnp.zeros((ROWS, META - 4 * TOPK), jnp.bfloat16))
    meta = jnp.concatenate(pieces, 1)
    cot_near = jnp.concatenate(gather_step(cotangent, stage_dims(0)), 0)
    cot_near = jnp.concatenate(gather_step(after(cot_near, pairs), stage_dims(1)), 0)
    cot_sides = gather_sides(cot_near)

    base = (ctx * tok_ctx).reshape(1)
    mixed = attend(base, queries, blocks, key_positions(tok_ctx), out_proj)
    mixed = lax.all_to_all(mixed, ("yl", "x"), 0, 0, tiled=True).reshape(8, ROWS, width)
    stream = resid.astype(jnp.float32) + jnp.sum(mixed.astype(jnp.float32), axis=0)
    normed = (
        stream * lax.rsqrt(jnp.mean(stream * stream, axis=1, keepdims=True) + 1e-06) * norm_gain
    ).astype(jnp.bfloat16)

    me = ctx.reshape(1)
    near = jnp.concatenate(
        gather_step(jnp.concatenate([normed, meta], 1), stage_dims(0)), 0
    )
    near = after(jnp.concatenate(gather_step(near, stage_dims(1)), 0), *cot_sides)
    left, right = gather_sides(near)
    half = near.shape[0] // 2
    narrow, wide = 2 * chunk, 4 * chunk

    slots = near.shape[0] // ROWS * CAP
    cuts = [slots // 32 * 16 + 16, slots // 32 * 16]
    thirds = [cuts[0], 2 * cuts[1], cuts[0]]

    def run_forward(rows_own, rows_got, backs):
        return forward(rows_own, rows_got, backs, w_gate, w_up, w_down, wide)

    own0, other0, place0, weight0 = pack_rows(me, [[near]], [slots], width, narrow)
    got0 = swap_cores(other0)
    out0, back0, hidden0 = run_forward(own0, got0, [slots])
    back0 = swap_cores(back0)
    left, right = after(left, out0), after(right, out0)

    far_a, far_b = gather_far(left, right)
    own1, other1, place1, weight1 = pack_rows(me, [[left], [right]], thirds, width, narrow)
    got1 = swap_cores(other1)
    (sum0,) = merge(place0, weight0, after(out0, *other1), back0, [(2 * half, 2 * half, 0)], narrow)
    out1, back1, hidden1 = run_forward(after(own1, sum0), got1, [2 * slots])
    back1 = swap_cores(back1)

    cot_left, cot_right = (after(side, far_a) for side in cot_sides)
    cot_far = gather_far(cot_left, cot_right)
    far_a, far_b = after(far_a, out1), after(far_b, out1)
    own2, other2, place2, weight2 = pack_rows(me, [[far_a, far_b]], cuts, width, narrow)
    got2 = swap_cores(other2)
    out2, back2, hidden2 = run_forward(own2, got2, cuts)
    back2 = swap_cores(back2)

    dims = stage_dims(2)
    left_a, left_b, right_a, right_b = merge(
        place1, weight1, after(out1, out2), back1, [(half, half, 0)] * 4, narrow
    )
    out2 = after(out2, left_a, *cot_far)
    far_a, far_b = merge(place2, weight2, out2, back2, [(half, half, 0)] * 2, narrow)
    got_far_a, got_far_b = send(far_a, dims, -1), send(far_b, dims, 1)
    got_left_b, got_right_a = send(left_b, dims, -1), send(right_a, dims, 1)

    cot_tiles = [[cot_near], [cot_left], [cot_right], list(cot_far)]
    places, weights = (place0, place1, place2), (weight0, weight1, weight2)
    grads_own, grads_other = pack_grads(places, weights, cot_tiles, chunk)
    grads = [grads_own] + swap_cores(after_all(grads_other, got_left_b, got_right_a))
    hiddens = [hidden0, hidden1, hidden2]

    left_a = add(left_a, got_far_a).astype(jnp.bfloat16)
    right_b = add(right_b, got_far_b).astype(jnp.bfloat16)
    got_left_a, got_right_b = send(left_a, dims, -1), send(right_b, dims, 1)
    back = back_act(grads, w_down, wide)
    total = jnp.concatenate(
        [
            add(sum0[:half], got_left_a, got_right_a),
            add(sum0[half:], got_left_b, got_right_b),
        ],
        0,
    )
    grad_down = down_grad(after_all(grads, back), hiddens, narrow)
    rows = [own0, own1, own2] + got0 + got1 + got2
    grad_gate, grad_up = up_grads(back, rows, hiddens, narrow)
    combined = scatter_near(total)
    layer_out = (stream + combined).astype(jnp.bfloat16)
    return layer_out, grad_gate, grad_up, grad_down


def solution(mesh):
    split = Mesh(mesh.devices.reshape(SIZES), AXES)
    ctx, tp = ("yh", "z", "k"), ("yl", "x")
    rows, weights = P(ctx + tp, None), P(ctx, tp, None)
    in_specs = (
        P(ctx, tp),
        P(ctx, None),
        P(ctx, None),
        rows,
        P(tp, None),
        P(),
        rows,
        rows,
        weights,
        weights,
        weights,
        rows,
    )
    return jax.shard_map(
        shards,
        mesh=split,
        in_specs=in_specs,
        out_specs=(rows, weights, weights, weights),
        check_vma=False,
    )
```

```python
import math

import jax
import jax.numpy as jnp
from jax import lax
from jax.experimental import pallas as pl
from jax.experimental.pallas import tpu as pltpu
from jax.sharding import Mesh
from jax.sharding import PartitionSpec as P

QHEADS = 32
KVHEADS = 2
HEAD = 128
TOPK = 8
CAP = 5
ROWS = 16
META = 128
SIZES = (2, 4, 2, 2, 4)
AXES = ("yh", "z", "k", "yl", "x")


def device_index(yh, z, k, yl, x):
    return (((yh * 4 + z) * 2 + k) * 2 + yl) * 4 + x


def shifted(dims, step):
    pairs = []
    for x in range(4):
        for y in range(4):
            for z in range(4):
                for k in range(2):
                    at = {"x": x, "y": y, "z": z}
                    to = dict(at)
                    to[dims[k]] = (to[dims[k]] + step) % 4
                    pairs.append(
                        (
                            device_index(at["y"] // 2, at["z"], k, at["y"] % 2, at["x"]),
                            device_index(to["y"] // 2, to["z"], k, to["y"] % 2, to["x"]),
                        )
                    )
    return pairs


def send(array, dims, step):
    return lax.ppermute(array, AXES, shifted(dims, step))


def swap_cores(arrays):
    return [lax.ppermute(array, "k", [(0, 1), (1, 0)]) for array in arrays]


def gather_step(block, dims):
    return [block, send(block, dims, 1), send(block, dims, -1), send(block, dims, 2)]


ORDERS = ("xyz", "zxy")


def stage_dims(stage):
    return (ORDERS[0][stage], ORDERS[1][stage])


def after(array, *others):
    return lax.optimization_barrier((array,) + others)[0]


def after_all(arrays, *others):
    return tuple(after(array, *others) for array in arrays)


def gather_near(block):
    for stage in range(2):
        block = jnp.concatenate(gather_step(block, stage_dims(stage)), 0)
    return block


def gather_sides(block):
    dims = stage_dims(2)
    return send(block, dims, 1), send(block, dims, -1)


def gather_far(left, right):
    dims = stage_dims(2)
    half = left.shape[0] // 2
    return send(left[:half], dims, 1), send(right[half:], dims, -1)


def add(*terms):
    total = terms[0].astype(jnp.float32)
    for term in terms[1:]:
        total = total + term.astype(jnp.float32)
    return total


def scatter_near(total):
    for stage in (1, 0):
        dims = stage_dims(stage)
        parts = total.astype(jnp.bfloat16).reshape(4, -1, total.shape[1])
        total = add(
            parts[0], send(parts[1], dims, -1), send(parts[2], dims, 1), send(parts[3], dims, -2)
        )
    return total


def placement(meta, experts, me):
    rows = meta.shape[0]
    slots = rows // ROWS * CAP
    turned = meta.astype(jnp.float32).T
    ids = turned[0:TOPK]
    gates = turned[TOPK : 2 * TOPK] + turned[2 * TOPK : 3 * TOPK] + turned[3 * TOPK : 4 * TOPK]
    token = lax.broadcasted_iota(jnp.int32, (rows, rows), 0)
    later = lax.broadcasted_iota(jnp.int32, (rows, rows), 1)
    earlier = ((token // ROWS == later // ROWS) & (token < later)).astype(jnp.float32)
    block = (lax.broadcasted_iota(jnp.int32, (1, rows), 1) // ROWS).astype(jnp.float32)
    slot_at = lax.broadcasted_iota(jnp.int32, (slots, rows), 0).astype(jnp.float32)
    places, weights = [], []
    for side in range(2):
        for local in range(experts):
            expert = ((me ^ side) * experts + local).astype(jnp.float32)
            named = ids == expert
            hit = jnp.max(named.astype(jnp.float32), axis=0, keepdims=True)
            gate = jnp.sum(jnp.where(named, gates, 0.0), axis=0, keepdims=True)
            rank = jnp.dot(
                jnp.broadcast_to(hit, (8, rows)), earlier, preferred_element_type=jnp.float32
            )[0:1]
            slot = jnp.where(hit > 0.0, block * CAP + rank, -1.0)
            place = (slot_at == slot).astype(jnp.float32)
            places.append(place)
            weights.append(jnp.sum(place * gate, axis=1, keepdims=True))
    return jnp.concatenate(places, 0), jnp.concatenate(weights, 0)


def cost(flops, *arrays):
    moved = sum(array.size * array.dtype.itemsize for array in arrays)
    return pl.CostEstimate(flops=int(flops), bytes_accessed=int(moved), transcendentals=0)


def call(kernel, grid, ins, in_specs, outs, out_specs, flops, scratch=(), limit=24, told=False):
    return pl.pallas_call(
        kernel,
        grid=grid,
        in_specs=in_specs,
        out_specs=out_specs,
        out_shape=outs,
        scratch_shapes=list(scratch),
        compiler_params=pltpu.CompilerParams(vmem_limit_bytes=limit * 1024 * 1024),
        cost_estimate=cost(flops, *ins, *outs) if told else None,
    )(*ins)


def shape(dims, dtype=jnp.bfloat16):
    return jax.ShapeDtypeStruct(dims, dtype)


def joined(refs):
    return refs[0][...] if len(refs) == 1 else jnp.concatenate([ref[...] for ref in refs], 0)


def store_slots(found, own_ref, other_refs):
    slots = found[0].shape[0] // 4
    for e in range(2):
        own_ref[e] = jnp.concatenate([tile[e * slots : (e + 1) * slots] for tile in found], 0)
        rows = jnp.concatenate([tile[(e + 2) * slots : (e + 3) * slots] for tile in found], 0)
        at = 0
        for ref in other_refs:
            ref[e] = rows[at : at + ref.shape[1]]
            at += ref.shape[1]


def pack_rows(me, groups, cuts, width, chunk):
    parts = [part for group in groups for part in group]
    tile_rows = sum(part.shape[0] for part in groups[0])
    slots = tile_rows // ROWS * CAP
    count, total = len(groups), len(parts)
    meta_at = width // META

    def kernel(me_ref, *refs):
        metas, rows = refs[:total], refs[total : 2 * total]
        own_ref, *other_refs, place_ref, weight_ref = refs[2 * total :]

        @pl.when(pl.program_id(0) == 0)
        def _():
            at = 0
            for tile, group in enumerate(groups):
                meta = joined(metas[at : at + len(group)])
                at += len(group)
                place, weight = placement(meta, 2, me_ref[0])
                place_ref[tile] = place.astype(jnp.bfloat16)
                weight_ref[tile] = jnp.broadcast_to(weight, weight_ref.shape[1:])

        at, found = 0, []
        for tile, group in enumerate(groups):
            block = joined(rows[at : at + len(group)])
            at += len(group)
            rows_of = jnp.dot(place_ref[tile], block, preferred_element_type=jnp.float32)
            found.append(rows_of.astype(jnp.bfloat16))
        store_slots(found, own_ref, other_refs)

    own, *others, place, weight = call(
        kernel,
        (width // chunk,),
        (me, *parts, *parts),
        [pl.BlockSpec(memory_space=pltpu.SMEM)]
        + [pl.BlockSpec((part.shape[0], META), lambda j: (0, meta_at)) for part in parts]
        + [pl.BlockSpec((part.shape[0], chunk), lambda j: (0, j)) for part in parts],
        [shape((2, count * slots, width))]
        + [shape((2, cut, width)) for cut in cuts]
        + [
            shape((count, 4 * slots, tile_rows)),
            shape((count, 4 * slots, META), jnp.float32),
        ],
        [pl.BlockSpec((2, count * slots, chunk), lambda j: (0, 0, j))]
        + [pl.BlockSpec((2, cut, chunk), lambda j: (0, 0, j)) for cut in cuts]
        + [
            pl.BlockSpec((count, 4 * slots, tile_rows), lambda j: (0, 0, 0)),
            pl.BlockSpec((count, 4 * slots, META), lambda j: (0, 0, 0)),
        ],
        2 * count * 4 * slots * tile_rows * width,
    )
    return own, others, place, weight


def pack_grads(places, weights, tiles, chunk):
    parts = [part for group in tiles for part in group]
    width = parts[0].shape[1]
    tile_rows = places[0].shape[2]
    slots = places[0].shape[1] // 4
    count = len(places)

    def kernel(*refs):
        place_refs, weight_refs = refs[:count], refs[count : 2 * count]
        rows = refs[2 * count : 2 * count + len(parts)]
        own_ref, *other_refs = refs[2 * count + len(parts) :]
        placed = [ref[t] for ref in place_refs for t in range(ref.shape[0])]
        scales = [ref[t] for ref in weight_refs for t in range(ref.shape[0])]
        at, found = 0, []
        for tile, group in enumerate(tiles):
            block = joined(rows[at : at + len(group)])
            at += len(group)
            rows_of = jnp.dot(placed[tile], block, preferred_element_type=jnp.float32)
            found.append((rows_of * scales[tile][:, 0:1]).astype(jnp.bfloat16))
        store_slots(found, own_ref, other_refs)

    own, *others = call(
        kernel,
        (width // chunk,),
        (*places, *weights, *parts),
        [pl.BlockSpec(a.shape, lambda j: (0, 0, 0)) for a in (*places, *weights)]
        + [pl.BlockSpec((part.shape[0], chunk), lambda j: (0, j)) for part in parts],
        [shape((2, len(tiles) * slots, width))] + [shape((2, slots, width))] * len(tiles),
        [pl.BlockSpec((2, len(tiles) * slots, chunk), lambda j: (0, 0, j))]
        + [pl.BlockSpec((2, slots, chunk), lambda j: (0, 0, j))] * len(tiles),
        2 * len(tiles) * 4 * slots * tile_rows * width,
        told=True,
    )
    return own, others


def merge(place, weight, own, others, pieces, chunk, into=()):
    width = own.shape[2]
    rows = place.shape[2]
    slots = place.shape[1] // 4
    count = own.shape[1] // slots

    def kernel(place_ref, weight_ref, own_ref, *refs):
        outs = refs[len(others) + len(into) :]
        other_rows = [
            jnp.concatenate([ref[e] for ref in refs[: len(others)]], 0) for e in range(2)
        ]
        totals = []
        for tile in range(count):
            span = pl.ds(tile * slots, slots)
            block = jnp.concatenate(
                [own_ref[e, span, :] for e in range(2)]
                + [rows_of[tile * slots : (tile + 1) * slots] for rows_of in other_rows],
                0,
            )
            scale = weight_ref[tile][:, 0:1]
            scaled = (block.astype(jnp.float32) * scale).astype(jnp.bfloat16)
            totals.append(t_dot(place_ref[tile], scaled).astype(jnp.bfloat16))
        at = 0
        for out, (size, _, _) in zip(outs, pieces):
            out[...] = totals[at // rows][at % rows : at % rows + size]
            at += size

    return pl.pallas_call(
        kernel,
        grid=(width // chunk,),
        in_specs=[
            pl.BlockSpec(place.shape, lambda j: (0, 0, 0)),
            pl.BlockSpec(weight.shape, lambda j: (0, 0, 0)),
            pl.BlockSpec((2, own.shape[1], chunk), lambda j: (0, 0, j)),
        ]
        + [pl.BlockSpec((2, other.shape[1], chunk), lambda j: (0, 0, j)) for other in others]
        + [pl.BlockSpec(memory_space=pl.ANY)] * len(into),
        out_specs=[
            pl.BlockSpec((size, chunk), lambda j, at=at: (at, j)) for size, _, at in pieces
        ],
        out_shape=[shape((total, width)) for _, total, _ in pieces],
        input_output_aliases={3 + len(others) + i: i for i in range(len(into))},
        compiler_params=pltpu.CompilerParams(vmem_limit_bytes=24 * 1024 * 1024),
    )(place, weight, own, *others, *into)


def dot_t(a, b):
    return lax.dot_general(a, b, (((1,), (1,)), ((), ())), preferred_element_type=jnp.float32)


def t_dot(a, b):
    return lax.dot_general(a, b, (((0,), (0,)), ((), ())), preferred_element_type=jnp.float32)


def forward(own, others, backs_cuts, w_gate, w_up, w_down, chunk):
    experts, rows, width = own.shape
    hidden = w_gate.shape[1]
    steps = width // chunk
    count = len(others)

    def kernel(own_ref, *refs):
        other_refs, (wg_ref, wu_ref, wd_ref) = refs[:count], refs[count : count + 3]
        own_out, *other_outs, hidden_ref, gate_sum, up_sum, active_ref = refs[count + 3 :]
        step = pl.program_id(1)

        @pl.when(step < steps)
        def _():
            block = jnp.concatenate([own_ref[0]] + [ref[0] for ref in other_refs], 0)
            gate = dot_t(block, wg_ref[0])
            up = dot_t(block, wu_ref[0])

            @pl.when(step == 0)
            def _():
                gate_sum[...] = gate
                up_sum[...] = up

            @pl.when(step > 0)
            def _():
                gate_sum[...] += gate
                up_sum[...] += up

        @pl.when(step == steps)
        def _():
            gate, up = gate_sum[...], up_sum[...]
            hidden_ref[0, 0] = gate
            hidden_ref[0, 1] = up
            active_ref[...] = (gate * jax.nn.sigmoid(gate) * up).astype(jnp.bfloat16)

        @pl.when(step >= steps)
        def _():
            out = jnp.dot(active_ref[...], wd_ref[0], preferred_element_type=jnp.float32)
            out = out.astype(jnp.bfloat16)
            own_out[0] = out[:rows]
            at = rows
            for other_out in other_outs:
                other_out[0] = out[at : at + other_out.shape[1]]
                at += other_out.shape[1]

    def early(e, s):
        return (e, 0, jnp.minimum(s, steps - 1))

    def late(e, s):
        return (e, 0, jnp.maximum(s - steps, 0))

    row_block = pl.BlockSpec((1, rows, chunk), early)
    weight_block = pl.BlockSpec((1, hidden, chunk), early)
    out, *backs, values = call(
        kernel,
        (experts, 2 * steps),
        (own, *others, w_gate, w_up, w_down),
        [row_block]
        + [pl.BlockSpec((1, other.shape[1], chunk), early) for other in others]
        + [weight_block, weight_block, pl.BlockSpec((1, hidden, chunk), late)],
        [shape(own.shape)] + [shape((experts, cut, width)) for cut in backs_cuts]
        + [shape((experts, 2, 2 * rows, hidden), jnp.float32)],
        [
            pl.BlockSpec((1, rows, chunk), late),
            *[pl.BlockSpec((1, cut, chunk), late) for cut in backs_cuts],
            pl.BlockSpec((1, 2, 2 * rows, hidden), lambda e, s: (e, 0, 0, 0)),
        ],
        12 * experts * rows * hidden * width,
        [
            pltpu.VMEM((2 * rows, hidden), jnp.float32),
            pltpu.VMEM((2 * rows, hidden), jnp.float32),
            pltpu.VMEM((2 * rows, hidden), jnp.bfloat16),
        ],
    )
    return out, backs, values


def back_act(grads, w_down, chunk):
    experts, _, width = grads[0].shape
    rows = sum(part.shape[1] for part in grads)
    hidden = w_down.shape[1]

    def kernel(*refs):
        wd_ref, out_ref = refs[-2:]
        found = dot_t(jnp.concatenate([ref[0] for ref in refs[:-2]], 0), wd_ref[0])

        @pl.when(pl.program_id(1) == 0)
        def _():
            out_ref[0] = found

        @pl.when(pl.program_id(1) > 0)
        def _():
            out_ref[0] += found

    return call(
        kernel,
        (experts, width // chunk),
        (*grads, w_down),
        [pl.BlockSpec((1, part.shape[1], chunk), lambda e, s: (e, 0, s)) for part in grads]
        + [pl.BlockSpec((1, hidden, chunk), lambda e, s: (e, 0, s))],
        [shape((experts, rows, hidden), jnp.float32)],
        [pl.BlockSpec((1, rows, hidden), lambda e, s: (e, 0, 0))],
        2 * experts * rows * hidden * width,
        told=True,
    )[0]


def hidden_of(refs, which):
    halves = [[], []]
    for ref in refs:
        rows = ref.shape[2] // 2
        for side in range(2):
            halves[side].append(ref[0, which, side * rows : (side + 1) * rows, :])
    return jnp.concatenate(halves[0] + halves[1], 0)


def down_grad(grads, hiddens, chunk):
    experts, _, width = grads[0].shape
    rows = sum(part.shape[1] for part in grads)
    units = hiddens[0].shape[3]
    count = len(grads)

    def kernel(*refs):
        hidden_refs, out_ref, active_ref = refs[count:-2], refs[-2], refs[-1]

        @pl.when(pl.program_id(1) == 0)
        def _():
            gate, up = hidden_of(hidden_refs, 0), hidden_of(hidden_refs, 1)
            active_ref[...] = (gate * jax.nn.sigmoid(gate) * up).astype(jnp.bfloat16)

        block = jnp.concatenate([ref[0] for ref in refs[:count]], 0)
        out_ref[0] = t_dot(active_ref[...], block).astype(jnp.bfloat16)

    return call(
        kernel,
        (experts, width // chunk),
        (*grads, *hiddens),
        [pl.BlockSpec((1, part.shape[1], chunk), lambda e, s: (e, 0, s)) for part in grads]
        + [pl.BlockSpec((1,) + h.shape[1:], lambda e, s: (e, 0, 0, 0)) for h in hiddens],
        [shape((experts, units, width))],
        [pl.BlockSpec((1, units, chunk), lambda e, s: (e, 0, s))],
        2 * experts * rows * units * width,
        [pltpu.VMEM((rows, units), jnp.bfloat16)],
        told=True,
    )[0]


def up_grads(back, ordered, hiddens, chunk):
    experts, rows, units = back.shape
    width = ordered[0].shape[2]
    count = len(ordered)

    def kernel(back_ref, *refs):
        row_refs, hidden_refs = refs[:count], refs[count:-4]
        dg_ref, du_ref, dgate, dup = refs[-4:]

        @pl.when(pl.program_id(1) == 0)
        def _():
            gate, up = hidden_of(hidden_refs, 0), hidden_of(hidden_refs, 1)
            sig = jax.nn.sigmoid(gate)
            d_act = back_ref[0]
            dgate[...] = (d_act * up * sig * (1.0 + gate * (1.0 - sig))).astype(jnp.bfloat16)
            dup[...] = (d_act * (gate * sig)).astype(jnp.bfloat16)

        block = jnp.concatenate([ref[0] for ref in row_refs], 0)
        dg_ref[0] = t_dot(dgate[...], block).astype(jnp.bfloat16)
        du_ref[0] = t_dot(dup[...], block).astype(jnp.bfloat16)

    out_block = pl.BlockSpec((1, units, chunk), lambda e, s: (e, 0, s))
    return call(
        kernel,
        (experts, width // chunk),
        (back, *ordered, *hiddens),
        [pl.BlockSpec((1, rows, units), lambda e, s: (e, 0, 0))]
        + [pl.BlockSpec((1, o.shape[1], chunk), lambda e, s: (e, 0, s)) for o in ordered]
        + [pl.BlockSpec((1,) + h.shape[1:], lambda e, s: (e, 0, 0, 0)) for h in hiddens],
        [shape((experts, units, width))] * 2,
        [out_block] * 2,
        4 * experts * rows * units * width,
        [pltpu.VMEM((rows, units), jnp.bfloat16)] * 2,
        told=True,
    )


def attend(base, queries, blocks, positions, out_proj):
    rows, width = queries.shape[0], out_proj.shape[1]
    tokens = positions.shape[1]
    steps = queries.shape[1] // (2 * HEAD)

    def kernel(base_ref, query_ref, first_ref, second_ref, pos_ref, proj_ref, out_ref, sum_ref):
        both = query_ref[...]
        query = jnp.concatenate([both[:, :HEAD], both[:, HEAD:]], 0)
        pairs = jnp.concatenate([first_ref[...], second_ref[...]], 0)
        scores = dot_t(query, pairs[:, :HEAD]) * (1.0 / math.sqrt(HEAD))
        query_pos = lax.broadcasted_iota(jnp.int32, (2 * rows, 1), 0) % rows + base_ref[0]
        scores = jnp.where(pos_ref[...] <= query_pos, scores, -1e30)
        probs = jnp.exp(scores - jnp.max(scores, axis=1, keepdims=True))
        denom = jnp.sum(probs, axis=1, keepdims=True)
        heads = jnp.dot(
            probs.astype(jnp.bfloat16), pairs[:, HEAD:], preferred_element_type=jnp.float32
        )
        heads = (heads / denom).astype(jnp.bfloat16)
        attn = jnp.concatenate([heads[:rows], heads[rows:]], 1)
        part = jnp.dot(attn, proj_ref[...], preferred_element_type=jnp.float32)
        step = pl.program_id(0)

        @pl.when(step == 0)
        def _():
            sum_ref[...] = part

        @pl.when(step > 0)
        def _():
            sum_ref[...] += part

        @pl.when(step == steps - 1)
        def _():
            out_ref[...] = sum_ref[...].astype(jnp.bfloat16)

    half = pl.BlockSpec((tokens // 2, 2 * HEAD), lambda h: (0, 0))
    return call(
        kernel,
        (steps,),
        (base, queries, *blocks, positions, out_proj),
        [
            pl.BlockSpec(memory_space=pltpu.SMEM),
            pl.BlockSpec((rows, 2 * HEAD), lambda h: (0, h)),
            half,
            half,
            pl.BlockSpec((1, tokens), lambda h: (0, 0)),
            pl.BlockSpec((2 * HEAD, width), lambda h: (h, 0)),
        ],
        [shape((rows, width))],
        [pl.BlockSpec((rows, width), lambda h: (0, 0))],
        2 * rows * queries.shape[1] * (2 * tokens + width),
        [pltpu.VMEM((rows, width), jnp.float32)],
        limit=56,
    )[0]


def key_positions(tok_ctx):
    k = lax.axis_index("k")
    groups = jnp.concatenate([2 * jnp.arange(8) + k, 2 * jnp.arange(8) + (1 - k)]).astype(jnp.int32)
    return (groups[:, None] * tok_ctx + jnp.arange(tok_ctx, dtype=jnp.int32)[None, :]).reshape(1, -1)


def shards(
    queries,
    keys,
    values,
    resid,
    out_proj,
    norm_gain,
    expert_ids,
    gates,
    w_gate,
    w_up,
    w_down,
    cotangent,
):
    width = resid.shape[1]
    chunk = min(512, width)
    yh, z, k, yl = (lax.axis_index(name) for name in ("yh", "z", "k", "yl"))
    ctx = ((yh * 4 + z) * 2 + k).astype(jnp.int32)

    tok_ctx = queries.shape[0]
    key_mine = lax.dynamic_slice_in_dim(keys, yl * HEAD, HEAD, 1)
    value_mine = lax.dynamic_slice_in_dim(values, yl * HEAD, HEAD, 1)
    pair = jnp.concatenate([key_mine, value_mine], 1)
    pairs = lax.all_to_all(
        jnp.broadcast_to(pair, (8,) + pair.shape), ("yh", "z"), 0, 0, tiled=True
    ).reshape(8 * tok_ctx, 2 * HEAD)
    blocks = [pairs] + swap_cores([pairs])

    rest = gates
    pieces = [expert_ids.astype(jnp.bfloat16)]
    for _ in range(3):
        piece = lax.reduce_precision(rest, 8, 7)
        pieces.append(piece.astype(jnp.bfloat16))
        rest = rest - piece
    pieces.append(jnp.zeros((ROWS, META - 4 * TOPK), jnp.bfloat16))
    meta = jnp.concatenate(pieces, 1)
    cot_near = jnp.concatenate(gather_step(cotangent, stage_dims(0)), 0)
    cot_near = jnp.concatenate(gather_step(after(cot_near, pairs), stage_dims(1)), 0)
    cot_sides = gather_sides(cot_near)

    base = (ctx * tok_ctx).reshape(1)
    mixed = attend(base, queries, blocks, key_positions(tok_ctx), out_proj)
    mixed = lax.all_to_all(mixed, ("yl", "x"), 0, 0, tiled=True).reshape(8, ROWS, width)
    stream = resid.astype(jnp.float32) + jnp.sum(mixed.astype(jnp.float32), axis=0)
    normed = (
        stream * lax.rsqrt(jnp.mean(stream * stream, axis=1, keepdims=True) + 1e-06) * norm_gain
    ).astype(jnp.bfloat16)

    me = ctx.reshape(1)
    near = jnp.concatenate(
        gather_step(jnp.concatenate([normed, meta], 1), stage_dims(0)), 0
    )
    near = after(jnp.concatenate(gather_step(near, stage_dims(1)), 0), *cot_sides)
    left, right = gather_sides(near)
    half = near.shape[0] // 2
    narrow, whole = 4 * chunk, 8 * chunk

    slots = near.shape[0] // ROWS * CAP
    cuts = [slots // 32 * 16 + 16, slots // 32 * 16]
    thirds = [cuts[0], 2 * cuts[1], cuts[0]]

    def run_forward(rows_own, rows_got, backs, cut):
        return forward(rows_own, rows_got, backs, w_gate, w_up, w_down, cut)

    own0, other0, place0, weight0 = pack_rows(me, [[near]], [slots], width, narrow)
    got0 = swap_cores(other0)
    out0, back0, hidden0 = run_forward(own0, got0, [slots], whole)
    back0 = swap_cores(back0)
    left, right = after(left, out0), after(right, out0)

    far_a, far_b = gather_far(left, right)
    own1, other1, place1, weight1 = pack_rows(me, [[left], [right]], thirds, width, narrow)
    got1 = swap_cores(other1)
    (sum0,) = merge(place0, weight0, after(out0, *other1), back0, [(2 * half, 2 * half, 0)], narrow)
    out1, back1, hidden1 = run_forward(after(own1, sum0), got1, [2 * slots], narrow)
    back1 = swap_cores(back1)

    cot_left, cot_right = (after(side, far_a) for side in cot_sides)
    cot_far = gather_far(cot_left, cot_right)
    far_a, far_b = after(far_a, out1), after(far_b, out1)
    own2, other2, place2, weight2 = pack_rows(me, [[far_a, far_b]], cuts, width, narrow)
    got2 = swap_cores(other2)
    out2, back2, hidden2 = run_forward(own2, got2, cuts, whole)
    back2 = swap_cores(back2)

    dims = stage_dims(2)
    left_a, left_b, right_a, right_b = merge(
        place1, weight1, after(out1, out2), back1, [(half, half, 0)] * 4, narrow
    )
    out2 = after(out2, left_a)
    far_a, far_b = merge(place2, weight2, out2, back2, [(half, half, 0)] * 2, narrow)
    got_far_a, got_far_b = send(far_a, dims, -1), send(far_b, dims, 1)
    left_b, right_a = after(left_b, *cot_far), after(right_a, *cot_far)
    got_left_b, got_right_a = send(left_b, dims, -1), send(right_a, dims, 1)

    cot_tiles = [[cot_near], [cot_left], [cot_right], list(cot_far)]
    places, weights = (place0, place1, place2), (weight0, weight1, weight2)
    grads_own, grads_other = pack_grads(places, weights, cot_tiles, 2 * chunk)
    grads = [grads_own] + swap_cores(after_all(grads_other, got_left_b, got_right_a))
    hiddens = [hidden0, hidden1, hidden2]

    left_a = add(left_a, got_far_a).astype(jnp.bfloat16)
    right_b = add(right_b, got_far_b).astype(jnp.bfloat16)
    got_left_a, got_right_b = send(left_a, dims, -1), send(right_b, dims, 1)
    back = back_act(grads, w_down, narrow)
    total = jnp.concatenate(
        [
            add(sum0[:half], got_left_a, got_right_a),
            add(sum0[half:], got_left_b, got_right_b),
        ],
        0,
    )
    grad_down = down_grad(after_all(grads, back), hiddens, narrow)
    rows = [own0, own1, own2] + got0 + got1 + got2
    grad_gate, grad_up = up_grads(back, rows, hiddens, narrow)
    combined = scatter_near(total)
    layer_out = (stream + combined).astype(jnp.bfloat16)
    return layer_out, grad_gate, grad_up, grad_down


def solution(mesh):
    split = Mesh(mesh.devices.reshape(SIZES), AXES)
    ctx, tp = ("yh", "z", "k"), ("yl", "x")
    rows, weights = P(ctx + tp, None), P(ctx, tp, None)
    in_specs = (
        P(ctx, tp),
        P(ctx, None),
        P(ctx, None),
        rows,
        P(tp, None),
        P(),
        rows,
        rows,
        weights,
        weights,
        weights,
        rows,
    )
    return jax.shard_map(
        shards,
        mesh=split,
        in_specs=in_specs,
        out_specs=(rows, weights, weights, weights),
        check_vma=False,
    )
```
